128 devices in a mesh: dp: 16 (over z, y), rep: 8 (over x, core).
Axes of the slice: x: 4, y: 4, z: 4, core: 2. Of those that a mesh axis runs over, the one named last changes fastest.
Arguments:
- hidden: bfloat16 [49152, 4096], P(('dp', 'rep')), may hold values from -6 to 6
- step_slot: int32 [49152], P(('dp', 'rep')), may hold values from 0 to 79, as said below
- positive: int32 [10240], P(('dp', 'rep')), may hold values from 0 to 10239, as said below
- proj: bfloat16 [4096, 1024], replicated, may hold values from -0.09375 to 0.09375
Outputs:
- hidden_grad: bfloat16 [49152, 4096], P(('dp', 'rep'))
- proj_grad: float32 [4096, 1024], P(('dp', 'rep'))
- loss: float32 [], replicated
The draws below stay inside these ranges and needn't reach their ends.
Inputs may be any that keep to these rules, and one draw needn't show every extreme that they name: `step_slot`: each solution owns 40 consecutive slots of its device and fills its first k of them, 2 <= k <= 40, with runs of consecutive tokens in order; some device has all its solutions at 40 steps. `positive`: for a live slot, another live slot of the same solution; for a slot that is not live, its own index.
All inputs are finite; a program needn't handle non-finite values.
Results may differ from the reference program's by a relative error of at most 0.0086.
Values may be sent and summed in bfloat16 or wider, within the bound.
A program may use at most 128 MiB of HBM per device.

```python
import math
import jax
import jax.numpy as jnp
from jax import lax

D = 4096
FEATURE_SIZE = 1024
SOL_DEV = 2
SOLUTION_LENGTH = 192
STEP_MAX = 40
TOK_DEV = 384
CAP = 80
SOLUTIONS = 256
TOKENS = 49152
STEPS = 10240
N_DP = 16
N_REP = 8


def layout(key):
    keys = jax.random.split(key, 3)
    owner = jnp.arange(SOLUTIONS, dtype=jnp.int32) // SOL_DEV
    steps = jax.random.randint(keys[0], (SOLUTIONS,), 2, STEP_MAX + 1).astype(jnp.int32)
    full_dev = jax.random.randint(keys[1], (), 0, SOLUTIONS // SOL_DEV).astype(jnp.int32)
    steps = jnp.where(owner == full_dev, STEP_MAX, steps)
    scores = jax.random.randint(keys[2], (SOLUTIONS, SOLUTION_LENGTH - 1), 0, 65536).astype(jnp.int32) * SOLUTION_LENGTH
    scores = scores + jnp.arange(SOLUTION_LENGTH - 1, dtype=jnp.int32)[None, :]
    ranks = jnp.argsort(jnp.argsort(scores, axis=1, stable=True), axis=1, stable=True).astype(jnp.int32)
    marks = (ranks < (steps - 1)[:, None]).astype(jnp.int32)
    step_id = jnp.concatenate([jnp.zeros((SOLUTIONS, 1), jnp.int32), jnp.cumsum(marks, axis=1).astype(jnp.int32)], axis=1)
    return (steps, step_id)


def draw_step_slot(key, part):
    steps, step_id = layout(key)
    within = jnp.arange(SOLUTIONS, dtype=jnp.int32) % SOL_DEV * STEP_MAX
    return (step_id + within[:, None]).reshape(TOKENS).astype(jnp.int32)


def draw_positive(key, part):
    steps, step_id = layout(key)
    key = jax.random.fold_in(key, 23)
    local = jnp.arange(STEP_MAX, dtype=jnp.int32)[None, :]
    offsets = jax.random.randint(key, (SOLUTIONS, STEP_MAX), 0, 4 * STEP_MAX).astype(jnp.int32) % (steps - 1)[:, None]
    partner = (local + 1 + offsets) % steps[:, None]
    base = jnp.arange(SOLUTIONS, dtype=jnp.int32)[:, None] * STEP_MAX
    selected_entries = jnp.where(local < steps[:, None], base + partner, base + local)
    return selected_entries.reshape(SOLUTIONS * STEP_MAX).astype(jnp.int32)


def level_of(rng, shape, shards, smallest, largest):
    level = 1.0
    for axis_at, shards_of in shards:
        steps = jax.random.uniform(jax.random.fold_in(jax.random.fold_in(rng, 6), axis_at), (shards_of,), jnp.float32, smallest / len(shards), largest / len(shards))
        level = level * jnp.repeat(jnp.exp(steps), shape[axis_at] // shards_of).reshape((-1,) + (1,) * (len(shape) - 1 - axis_at))
    return level


def gaussian(stream_key, dims, spread, reach, cuts=(), kind=jnp.bfloat16):
    factor_of = level_of(stream_key, dims, cuts, -0.22, 0.18) if cuts else 1.0
    drawn = jax.random.normal(stream_key, dims, jnp.float32) * spread * factor_of
    return jnp.minimum(jnp.maximum(drawn, -reach), reach).astype(kind)


def setup_inputs(seed: int = 0) -> dict:
    key_list = jax.random.split(jax.random.key(seed), 5)
    return {
        "hidden": gaussian(key_list[0], (TOKENS, D), 1.0, 6.0, ((0, 128),)),
        "step_slot": draw_step_slot(jax.random.fold_in(key_list[4], 71), 0),
        "positive": draw_positive(jax.random.fold_in(key_list[4], 71), 0),
        "proj": gaussian(key_list[3], (D, FEATURE_SIZE), D ** -0.5, 0.09375),
    }


sharpness_divisor = 0.3

def reference(hidden, step_slot, positive, proj):
    devices = N_DP * N_REP
    slots = jnp.arange(CAP, dtype=jnp.int32)

    def pool_one(args):
        rows, where_slot = args
        member = where_slot[None, :] == slots[:, None]
        step_counts = lax.optimization_barrier(jnp.sum(member.astype(jnp.int32), axis=1))
        sums = jnp.dot(member.astype(jnp.bfloat16), rows, preferred_element_type=jnp.float32)
        denom = jnp.maximum(step_counts, 1).astype(jnp.float32)
        return ((sums / denom[:, None]).astype(jnp.bfloat16), step_counts)
    pooled, step_counts = lax.map(pool_one, (hidden.reshape(devices, TOK_DEV, D), step_slot.reshape(devices, TOK_DEV)))
    pooled = pooled.reshape(STEPS, D)
    step_counts = step_counts.reshape(STEPS)
    denom = jnp.maximum(step_counts, 1).astype(jnp.float32)
    embed = jnp.dot(pooled, proj, preferred_element_type=jnp.float32)
    reciprocal_scale = lax.rsqrt(lax.optimization_barrier(jnp.mean(embed * embed, axis=1)) + 1e-06)
    unit = embed * reciprocal_scale[:, None]
    unit_b = unit.astype(jnp.bfloat16)
    similarity_multiplier = 1.0 / (sharpness_divisor * math.sqrt(FEATURE_SIZE))
    scores = jnp.dot(unit_b, unit_b.T, preferred_element_type=jnp.float32) * similarity_multiplier
    live = step_counts > 0
    ids = jnp.arange(STEPS, dtype=jnp.int32)
    mask = live[None, :] & (ids[None, :] != ids[:, None])
    lse = jnp.log(lax.optimization_barrier(jnp.sum(jnp.where(mask, jnp.exp(scores), 0.0), axis=1)))
    nlive = jnp.sum(live.astype(jnp.float32))
    onepos = (ids[None, :] == positive[:, None]).astype(jnp.float32)
    spos = lax.optimization_barrier(jnp.sum(scores * onepos, axis=1))
    loss = jnp.sum(jnp.where(live, lse - spos, 0.0)) / nlive
    probs = jnp.where(mask, jnp.exp(scores - lse[:, None]), 0.0)
    grad_raw = jnp.where(live[:, None], probs - onepos, 0.0)
    pair_weight = ((grad_raw + grad_raw.T) / nlive).astype(jnp.bfloat16)
    unit_grad = jnp.dot(pair_weight, unit_b, preferred_element_type=jnp.float32) * similarity_multiplier
    inner = lax.optimization_barrier(jnp.mean(unit * unit_grad, axis=1, keepdims=True))
    embed_grad = (reciprocal_scale[:, None] * (unit_grad - unit * inner)).astype(jnp.bfloat16)
    proj_grad = lax.dot_general(pooled, embed_grad, (((0,), (0,)), ((), ())), preferred_element_type=jnp.float32)
    pooled_grad = lax.dot_general(embed_grad, proj, (((1,), (1,)), ((), ())), preferred_element_type=jnp.float32)
    pooled_grad = (pooled_grad / denom[:, None]).astype(jnp.bfloat16)

    def spread_one(args):
        where_slot, grads = args
        member = (where_slot[None, :] == slots[:, None]).astype(jnp.bfloat16)
        out = lax.dot_general(member, grads, (((0,), (0,)), ((), ())), preferred_element_type=jnp.float32)
        return out.astype(jnp.bfloat16)
    hidden_grad = lax.map(spread_one, (step_slot.reshape(devices, TOK_DEV), pooled_grad.reshape(devices, CAP, D)))
    return (hidden_grad.reshape(TOKENS, D), proj_grad, loss)
```

```python
import functools
import math

import jax
import jax.numpy as jnp
from jax import lax
from jax.experimental import pallas as pl
from jax.experimental.pallas import tpu as pltpu
from jax.sharding import PartitionSpec as P

MESH = pl.DeviceIdType.MESH
F32 = jnp.float32
BF16 = jnp.bfloat16
CAP = 80
TOK = 384
D = 4096
F = 1024
ROWS = 640
COLS = 1280
EXTRA = COLS + 128
MULT = 1.0 / (0.3 * math.sqrt(F))
LOG2E = 1.4426950408889634
NEG = -1e30
MARK = 256.0


def rcopy(src, dst, send_sem, recv_sem, device):
    return pltpu.make_async_remote_copy(
        src_ref=src, dst_ref=dst, send_sem=send_sem, recv_sem=recv_sem, device_id=device, device_id_type=MESH
    )


class GatherDp:
    def __init__(self, buf, ssem, rsem, z, y, rep):
        self.buf, self.ssem, self.rsem = buf, ssem, rsem
        self.z = [z, (z + 1) % 4, (z + 2) % 4, (z + 3) % 4]
        self.y = [y, (y + 1) % 4, (y + 2) % 4, (y + 3) % 4]
        self.dev = [
            (self.z[1] * 4 + y, rep),
            (self.z[3] * 4 + y, rep),
            (z * 4 + self.y[1], rep),
            (z * 4 + self.y[3], rep),
        ]
        self.copies = {}

    def send(self, direction, slot, h, d, dz, dy):
        at = pl.ds(pl.multiple_of((self.z[dz % 4] * 4 + self.y[dy % 4]) * CAP, CAP), CAP)
        piece = self.buf.at[h, d, at]
        c = rcopy(piece, piece, self.ssem.at[direction, slot], self.rsem.at[direction, slot], self.dev[direction])
        c.start()
        self.copies[direction, slot] = c

    def recv(self, *which):
        for w in which:
            self.copies[w].wait_recv()

    def round1(self):
        a = slice(None)
        for direction in range(4):
            self.send(direction, 0, a, a, 0, 0)

    def round2(self):
        a = slice(None)
        self.recv((0, 0))
        self.send(0, 1, a, 0, -1, 0)
        self.send(2, 2, 0, a, -1, 0)
        self.send(3, 2, 0, a, -1, 0)
        self.recv((2, 0))
        self.send(2, 1, a, 0, 0, -1)
        self.send(0, 2, 1, a, 0, -1)
        self.send(1, 2, 1, a, 0, -1)
        self.recv((1, 0))
        self.send(1, 1, a, 1, 1, 0)
        self.send(2, 3, 0, a, 1, 0)
        self.send(3, 3, 0, a, 1, 0)
        self.recv((3, 0))
        self.send(3, 1, a, 1, 0, 1)
        self.send(0, 3, 1, a, 0, 1)
        self.send(1, 3, 1, a, 0, 1)

    def round3(self):
        a = slice(None)
        self.recv((0, 1), (1, 1))
        self.send(2, 4, 0, a, 2, 0)
        self.send(3, 4, 0, a, 2, 0)
        self.recv((2, 1), (3, 1))
        self.send(0, 4, 1, a, 0, 2)
        self.send(1, 4, 1, a, 0, 2)
        self.recv((0, 2))
        self.send(0, 5, 1, 0, -1, -1)
        self.recv((2, 2))
        self.send(2, 5, 0, 0, -1, -1)
        self.recv((1, 2))
        self.send(1, 5, 1, 1, 1, -1)
        self.recv((3, 2))
        self.send(3, 5, 0, 1, -1, 1)
        self.recv((0, 3))
        self.send(0, 6, 1, 0, -1, 1)
        self.recv((2, 3))
        self.send(2, 6, 0, 0, 1, -1)
        self.recv((1, 3))
        self.send(1, 6, 1, 1, 1, 1)
        self.recv((3, 3))
        self.send(3, 6, 0, 1, 1, 1)

    def round4(self):
        self.recv((0, 4))
        self.send(0, 7, 1, 0, -1, 2)
        self.recv((1, 4))
        self.send(1, 7, 1, 1, 1, 2)
        self.recv((2, 4))
        self.send(2, 7, 0, 0, 2, -1)
        self.recv((3, 4))
        self.send(3, 7, 0, 1, 2, 1)

    def finish(self):
        for slot in (5, 6, 7):
            for direction in range(4):
                self.recv((direction, slot))

    def drain(self):
        for c in self.copies.values():
            c.wait_send()


class GatherRep:
    def __init__(self, buf, ssem, rsem, dp, x, k):
        self.buf, self.ssem, self.rsem, self.k = buf, ssem, rsem, k
        self.x = [x, (x + 1) % 4, (x + 2) % 4, (x + 3) % 4]
        self.dev = [(dp, self.x[1] * 2 + k), (dp, self.x[3] * 2 + k), (dp, x * 2 + 1 - k)]
        self.copies = {}

    def send(self, direction, slot, u, dx):
        at = pl.ds(pl.multiple_of((self.x[dx % 4] * 2 + self.k) * CAP, CAP), CAP)
        piece = self.buf.at[u, :, at]
        c = rcopy(piece, piece, self.ssem.at[direction, slot], self.rsem.at[direction, slot], self.dev[direction])
        c.start()
        self.copies[direction, slot] = c

    def recv(self, *which):
        for w in which:
            self.copies[w].wait_recv()

    def round1(self):
        for direction in range(3):
            self.send(direction, 0, slice(None), 0)

    def round2(self):
        self.recv((0, 0))
        self.send(0, 1, 0, -1)
        self.send(2, 1, slice(None), -1)
        self.recv((1, 0))
        self.send(1, 1, 1, 1)
        self.send(2, 2, slice(None), 1)

    def round3(self):
        self.recv((0, 1))
        self.send(2, 3, 0, 2)
        self.recv((1, 1))
        self.send(2, 4, 1, 2)

    def finish(self):
        for slot in range(5):
            self.recv((2, slot))

    def drain(self):
        for c in self.copies.values():
            c.wait_send()


class ReduceRep:
    def __init__(self, full, out, sib, far, far_in, near, near_in, mid, mid_in, ssem, rsem, dp, x, k):
        self.full, self.out, self.sib = full, out, sib
        self.far, self.far_in, self.near, self.near_in, self.mid, self.mid_in = far, far_in, near, near_in, mid, mid_in
        self.ssem, self.rsem, self.k = ssem, rsem, k
        self.x = [x, (x + 1) % 4, (x + 2) % 4, (x + 3) % 4]
        self.right, self.left = (dp, self.x[1] * 2 + k), (dp, self.x[3] * 2 + k)
        self.other = (dp, x * 2 + 1 - k)
        self.copies = {}

    def send(self, kind, q, src, dst, device):
        c = rcopy(src, dst, self.ssem.at[kind, q], self.rsem.at[kind, q], device)
        c.start()
        self.copies[kind, q] = c

    def put(self, q, value):
        parts = value.reshape((4, 2) + (value.shape[0] // 8, 256))
        self.full[q] = parts
        self.out[q] = parts.astype(self.out.dtype)
        self.send(0, q, self.out.at[q, :, 1 - self.k], self.sib.at[q], self.other)

    def part(self, q, dx):
        at = self.x[dx % 4]
        return self.full[q, at, self.k] + self.sib[q, at].astype(F32)

    def step1(self, q):
        self.copies[0, q].wait_recv()
        ahead, behind = (self.right, self.left) if q < 2 else (self.left, self.right)
        self.far[q] = self.part(q, 2).astype(self.far.dtype)
        self.send(1, q, self.far.at[q], self.far_in.at[q], ahead)
        self.near[q] = self.part(q, -1 if q < 2 else 1).astype(self.near.dtype)
        self.send(2, q, self.near.at[q], self.near_in.at[q], behind)

    def step2(self, q):
        self.copies[1, q].wait_recv()
        self.mid[q] = (self.part(q, 1 if q < 2 else -1) + self.far_in[q].astype(F32)).astype(self.mid.dtype)
        self.send(3, q, self.mid.at[q], self.mid_in.at[q], self.right if q < 2 else self.left)

    def result(self, q):
        self.copies[2, q].wait_recv()
        self.copies[3, q].wait_recv()
        return self.part(q, 0) + self.near_in[q].astype(F32) + self.mid_in[q].astype(F32)

    def drain(self):
        for c in self.copies.values():
            c.wait_send()


ORDER = (0, 2, 1, 3)


def kernel(
    hidden_hbm, slot_ref, pos_ref, proj_hbm,
    pgrad_out, proj_out, loss_out,
    hid, proj, pooled, pooled_in, pooled_t, uc, ur, ec, scores, weights, rowsum, zc, zr, zl, bias_c,
    posterm, unit_s,
    g_full, g_out, g_sib, g_far, g_far_in, g_near, g_near_in, g_mid, g_mid_in,
    p_full, p_out, p_sib, p_far, p_far_in, p_near, p_near_in, p_mid, p_mid_in,
    load_sem, uc_s, uc_r, ur_s, ur_r, ec_s, ec_r, g_s, g_r, p_s, p_r, a2a_s, a2a_r, zc_s, zc_r, zr_s, zr_r, zl_s, zl_r,
):
    dp, rep = lax.axis_index("dp"), lax.axis_index("rep")
    z, y, x, k = dp // 4, dp % 4, rep // 2, rep % 2
    dp_peers = [((dp + j) % 16, rep) for j in range(1, 16)]
    rep_peers = [(dp, (rep + j) % 8) for j in range(1, 8)]

    loads = []
    for j in range(4):
        loads.append(
            (
                pltpu.make_async_copy(hidden_hbm.at[:, pl.ds(j * 1024, 1024)], hid.at[j], load_sem.at[0, j]),
                pltpu.make_async_copy(proj_hbm.at[pl.ds(j * 1024, 1024)], proj.at[pl.ds(j * 1024, 1024)], load_sem.at[1, j]),
            )
        )
        loads[-1][0].start()
        loads[-1][1].start()

    barrier = pltpu.get_barrier_semaphore()
    for peer in dp_peers + rep_peers:
        pl.semaphore_signal(barrier, inc=1, device_id=peer, device_id_type=MESH)

    member = slot_ref[...] == lax.broadcasted_iota(jnp.int32, (CAP, TOK), 0)
    onehot = member.astype(F32)
    counts = jnp.sum(onehot, axis=1, keepdims=True)
    onehot = onehot.astype(BF16)
    denom = jnp.maximum(counts, 1.0)
    live = counts > 0.0
    embed = jnp.zeros((CAP, F), F32)
    for j in range(4):
        loads[j][0].wait()
        chunk = (jnp.dot(onehot, hid[j], preferred_element_type=F32) / denom).astype(BF16)
        for i in range(4):
            pooled[j * 4 + i] = chunk[:, i * 256 : (i + 1) * 256]
        loads[j][1].wait()
        embed = embed + jnp.dot(chunk, proj[pl.ds(j * 1024, 1024), :], preferred_element_type=F32)
    rscale = lax.rsqrt(jnp.mean(embed * embed, axis=1, keepdims=True) + 1e-06)
    unit = embed * rscale
    unit_s[...] = unit
    unit_b = unit.astype(BF16)
    lane = lax.broadcasted_iota(jnp.int32, (CAP, F), 1)
    marked = jnp.where(jnp.logical_and(lane == 0, jnp.logical_not(live)), MARK, unit).astype(BF16)
    at_c = pl.ds(pl.multiple_of(dp * CAP, CAP), CAP)
    at_r = pl.ds(pl.multiple_of(rep * CAP, CAP), CAP)
    for q in range(4):
        piece = marked[:, q * 256 : (q + 1) * 256]
        uc[q // 2, q % 2, at_c, :] = piece
        ur[q // 2, q % 2, at_r, :] = piece

    pl.semaphore_wait(barrier, 22)

    gc = GatherDp(uc, uc_s, uc_r, z, y, rep)
    gr = GatherRep(ur, ur_s, ur_r, dp, x, k)
    gc.round1()
    gr.round1()

    at_pos = pos_ref[...] - (dp * 8 + rep) * CAP
    row80 = lax.broadcasted_iota(jnp.int32, (CAP, CAP), 0)
    col80 = lax.broadcasted_iota(jnp.int32, (CAP, CAP), 1)
    back = jnp.where(jnp.logical_and(at_pos == row80, row80 != col80), 1.0, 0.0).astype(BF16)
    partner = lax.dot_general(back, unit_b, (((0,), (0,)), ((), ())), preferred_element_type=F32)
    posterm[...] = partner + jnp.dot(back, unit_b, preferred_element_type=F32)
    picked = jnp.sum(jnp.sum(partner * unit_b.astype(F32), axis=1, keepdims=True), axis=0, keepdims=True) * MULT

    gr.round2()
    gc.round2()
    gr.round3()
    gc.round3()
    gc.round4()
    gr.finish()
    gc.finish()

    a2a = []
    for j in range(15):
        peer = dp_peers[j]
        c = rcopy(pooled.at[peer[0]], pooled_in.at[pl.ds(pl.multiple_of(dp * CAP, CAP), CAP)], a2a_s.at[j], a2a_r.at[j], peer)
        c.start()
        a2a.append(c)
    pooled_in[at_c, :] = pooled[dp]

    rows = jnp.concatenate([ur[q // 2, q % 2] for q in range(4)], axis=1)
    live_r = ur[0, 0, :, 0:1].astype(F32) < 128.0
    bias_r = jnp.where(live_r, 0.0, NEG)
    nlive_r = jnp.sum(jnp.where(live_r, 1.0, 0.0), axis=0, keepdims=True)
    id_r = lax.broadcasted_iota(jnp.int32, (ROWS, 1), 0) - rep * CAP
    id_r = jnp.where(jnp.logical_and(id_r >= 0, id_r < CAP), id_r, -1)
    pick0 = jnp.where(lax.broadcasted_iota(jnp.int32, (16, 256), 1) == 0, 1.0, 0.0).astype(BF16)
    rowsum[...] = jnp.zeros_like(rowsum)

    def score_tile(t, carry):
        at = pl.ds(pl.multiple_of(t * 256, 256), 256)
        cols = jnp.concatenate([uc[q // 2, q % 2, at, :] for q in range(4)], axis=1)
        first = lax.dot_general(pick0, cols[:, :256], (((1,), (1,)), ((), ())), preferred_element_type=F32)
        bias = jnp.where(first[0:1] < 128.0, 0.0, NEG)
        bias_c[:, at] = bias
        id_c = lax.broadcasted_iota(jnp.int32, (1, 256), 1) + t * 256 - dp * CAP
        id_c = jnp.where(jnp.logical_and(id_c >= 0, id_c < CAP), id_c, -2)
        s = lax.dot_general(rows, cols, (((1,), (1,)), ((), ())), preferred_element_type=F32) * (MULT * LOG2E)
        s = jnp.where(id_r == id_c, NEG, s + bias_r + bias)
        scores[:, at] = s
        e = jnp.exp2(s)
        zc[dp, :, at] = jnp.sum(e, axis=0, keepdims=True)
        rowsum[...] += e[:, :128] + e[:, 128:]
        return carry

    lax.fori_loop(0, 5, score_tile, 0)
    zr[rep] = jnp.sum(rowsum[...].T, axis=0, keepdims=True)
    l128 = lax.broadcasted_iota(jnp.int32, (1, 128), 1)
    zc[dp, :, pl.ds(COLS, 128)] = jnp.where(l128 == 0, nlive_r, jnp.where(l128 == 1, picked, 0.0))

    zcopies = []
    for j in range(15):
        zcopies.append(rcopy(zc.at[dp], zc.at[dp], zc_s.at[j], zc_r.at[j], dp_peers[j]))
        zcopies[-1].start()
    for j in range(7):
        zcopies.append(rcopy(zr.at[rep], zr.at[rep], zr_s.at[j], zr_r.at[j], rep_peers[j]))
        zcopies[-1].start()
    for c in zcopies:
        c.wait_recv()

    total_c = zc[0]
    for j in range(1, 16):
        total_c = total_c + zc[j]
    total_r = zr[0]
    for j in range(1, 8):
        total_r = total_r + zr[j]
    nlive = total_c[:, COLS : COLS + 1]
    log_c = jnp.where(bias_c[...] < -1.0, 0.0, jnp.log(total_c[:, :COLS]))
    loss_c = jnp.sum(log_c, axis=1, keepdims=True) - total_c[:, COLS + 1 : COLS + 2]
    zl[rep] = jnp.broadcast_to(loss_c, (1, 128))
    lcopies = []
    for j in range(7):
        lcopies.append(rcopy(zl.at[rep], zl.at[rep], zl_s.at[j], zl_r.at[j], rep_peers[j]))
        lcopies[-1].start()
    bias_c[...] = log_c * LOG2E
    log_r = jnp.broadcast_to(jnp.log(total_r) * LOG2E, (128, ROWS)).T
    log_r = jnp.where(live_r, log_r, 0.0)
    rowsum[...] = log_r

    def weight_tile(t, carry):
        at = pl.ds(pl.multiple_of(t * 128, 128), 128)
        s = scores[:, at]
        w = jnp.exp2(s - rowsum[...]) + jnp.exp2(s - bias_c[:, at])
        weights[:, at] = w.astype(BF16)
        return carry

    lax.fori_loop(0, 10, weight_tile, 0)

    red = ReduceRep(g_full, g_out, g_sib, g_far, g_far_in, g_near, g_near_in, g_mid, g_mid_in, g_s, g_r, dp, x, k)
    for q in ORDER:
        red.put(q, jnp.dot(weights[...], uc[q // 2, q % 2], preferred_element_type=F32))
    for q in ORDER:
        red.step1(q)
    for q in ORDER:
        red.step2(q)
    got = jnp.concatenate([red.result(q) for q in range(4)], axis=1)
    unit = unit_s[...]
    ugrad = (got - posterm[...]) * (MULT / nlive)
    inner = jnp.mean(unit * ugrad, axis=1, keepdims=True)
    egrad = (rscale * (ugrad - unit * inner)).astype(BF16)
    for q in range(4):
        ec[q // 2, q % 2, at_c, :] = egrad[:, q * 256 : (q + 1) * 256]

    ge = GatherDp(ec, ec_s, ec_r, z, y, rep)

    def pgrad(j):
        at = pl.ds(j * 512, 512)
        part = lax.dot_general(egrad, proj[at, :], (((1,), (1,)), ((), ())), preferred_element_type=F32)
        pgrad_out[:, at] = (part / denom).astype(BF16)

    ge.round1()
    for c in a2a:
        c.wait_recv()
    pooled_t[...] = pooled_in[...].astype(F32).T.astype(BF16)
    pgrad(0)
    ge.round2()
    pgrad(1)
    pgrad(2)
    ge.round3()
    pgrad(3)
    pgrad(4)
    ge.round4()
    for j in range(5, 8):
        pgrad(j)
    ge.finish()

    red2 = ReduceRep(p_full, p_out, p_sib, p_far, p_far_in, p_near, p_near_in, p_mid, p_mid_in, p_s, p_r, dp, x, k)
    for q in ORDER:
        red2.put(q, jnp.dot(pooled_t[...], ec[q // 2, q % 2], preferred_element_type=F32))
    for q in ORDER:
        red2.step1(q)
    for q in ORDER:
        red2.step2(q)
    for q in range(4):
        proj_out[:, q * 256 : (q + 1) * 256] = red2.result(q)

    for c in lcopies:
        c.wait_recv()
    loss = zl[0]
    for j in range(1, 8):
        loss = loss + zl[j]
    loss_out[...] = loss / nlive

    for group in (gc, gr, red, ge, red2):
        group.drain()
    for c in a2a + zcopies + lcopies:
        c.wait_send()


def reduce_scratch(n, kind):
    return [pltpu.VMEM((4, 4, 2, n, 256), F32), pltpu.VMEM((4, 4, 2, n, 256), kind), pltpu.VMEM((4, 4, n, 256), kind)] + [
        pltpu.VMEM((4, n, 256), kind) for _ in range(6)
    ]


def local(hidden, step_slot, positive, proj):
    dma = pltpu.SemaphoreType.DMA
    vm = pl.BlockSpec(memory_space=pltpu.VMEM)
    hbm = pl.BlockSpec(memory_space=pl.ANY)
    pooled_grad, proj_grad, loss = pl.pallas_call(
        kernel,
        out_shape=(
            jax.ShapeDtypeStruct((CAP, D), BF16),
            jax.ShapeDtypeStruct((32, F), F32),
            jax.ShapeDtypeStruct((1, 128), F32),
        ),
        in_specs=[hbm, vm, vm, hbm],
        out_specs=(vm, vm, vm),
        scratch_shapes=[
            pltpu.VMEM((4, TOK, 1024), BF16),
            pltpu.VMEM((D, F), BF16),
            pltpu.VMEM((16, CAP, 256), BF16),
            pltpu.VMEM((COLS, 256), BF16),
            pltpu.VMEM((256, COLS), BF16),
            pltpu.VMEM((2, 2, COLS, 256), BF16),
            pltpu.VMEM((2, 2, ROWS, 256), BF16),
            pltpu.VMEM((2, 2, COLS, 256), BF16),
            pltpu.VMEM((ROWS, COLS), F32),
            pltpu.VMEM((ROWS, COLS), BF16),
            pltpu.VMEM((ROWS, 128), F32),
            pltpu.VMEM((16, 1, EXTRA), F32),
            pltpu.VMEM((8, 1, ROWS), F32),
            pltpu.VMEM((8, 1, 128), F32),
            pltpu.VMEM((1, COLS), F32),
            pltpu.VMEM((CAP, F), F32),
            pltpu.VMEM((CAP, F), F32),
        ]
        + reduce_scratch(CAP, BF16)
        + reduce_scratch(32, BF16)
        + [
            dma((2, 4)),
            dma((4, 8)), dma((4, 8)), dma((3, 5)), dma((3, 5)), dma((4, 8)), dma((4, 8)),
            dma((4, 4)), dma((4, 4)), dma((4, 4)), dma((4, 4)),
            dma((15,)), dma((15,)), dma((15,)), dma((15,)), dma((7,)), dma((7,)), dma((7,)), dma((7,)),
        ],
        compiler_params=pltpu.CompilerParams(
            collective_id=0, has_side_effects=True, vmem_limit_bytes=60 * 1024 * 1024
        ),
        cost_estimate=pl.CostEstimate(flops=6_000_000_000, bytes_accessed=14_000_000, transcendentals=2_000_000),
    )(hidden, step_slot.reshape(1, TOK), positive.reshape(1, CAP), proj)
    onehot = (step_slot[None, :] == lax.broadcasted_iota(jnp.int32, (CAP, TOK), 0)).astype(BF16)
    hidden_grad = lax.dot_general(onehot, pooled_grad, (((0,), (0,)), ((), ())), preferred_element_type=F32)
    return (hidden_grad.astype(BF16), proj_grad, loss[0, 0])


def solution(mesh):
    in_specs = (P(("dp", "rep"), None), P(("dp", "rep")), P(("dp", "rep")), P())
    out_specs = (P(("dp", "rep"), None), P(("dp", "rep"), None), P())
    return jax.shard_map(local, mesh=mesh, in_specs=in_specs, out_specs=out_specs, check_vma=False)
```

```python
import functools
import math

import jax
import jax.numpy as jnp
from jax import lax
from jax.experimental import pallas as pl
from jax.experimental.pallas import tpu as pltpu
from jax.sharding import PartitionSpec as P

MESH = pl.DeviceIdType.MESH
F32 = jnp.float32
BF16 = jnp.bfloat16
CAP = 80
TOK = 384
D = 4096
F = 1024
ROWS = 640
COLS = 1280
EXTRA = COLS + 128
MULT = 1.0 / (0.3 * math.sqrt(F))
LOG2E = 1.4426950408889634
NEG = -1e30
MARK = 256.0


def rcopy(src, dst, send_sem, recv_sem, device):
    return pltpu.make_async_remote_copy(
        src_ref=src, dst_ref=dst, send_sem=send_sem, recv_sem=recv_sem, device_id=device, device_id_type=MESH
    )


class GatherDp:
    def __init__(self, buf, ssem, rsem, z, y, rep):
        self.buf, self.ssem, self.rsem = buf, ssem, rsem
        self.z = [z, (z + 1) % 4, (z + 2) % 4, (z + 3) % 4]
        self.y = [y, (y + 1) % 4, (y + 2) % 4, (y + 3) % 4]
        self.dev = [
            (self.z[1] * 4 + y, rep),
            (self.z[3] * 4 + y, rep),
            (z * 4 + self.y[1], rep),
            (z * 4 + self.y[3], rep),
        ]
        self.copies = {}

    def at(self, dz, dy):
        return pl.ds(pl.multiple_of((self.z[dz % 4] * 4 + self.y[dy % 4]) * CAP, CAP), CAP)

    def send(self, direction, slot, h, d, dz, dy):
        piece = self.buf.at[h, d, self.at(dz, dy)]
        c = rcopy(piece, piece, self.ssem.at[direction, slot], self.rsem.at[direction, slot], self.dev[direction])
        c.start()
        self.copies[direction, slot] = c

    def recv(self, *which):
        for w in which:
            self.copies[w].wait_recv()

    def start(self, h):
        a = slice(None)
        for direction in (0, 1) if h == 0 else (2, 3):
            self.send(direction, 0, h, a, 0, 0)
        for direction in (2, 3) if h == 0 else (0, 1):
            self.send(direction, 8, h, a, 0, 0)

    def first(self, h):
        a = slice(None)
        if h == 0:
            self.recv((0, 0))
            self.send(0, 1, 0, 0, -1, 0)
            self.send(2, 2, 0, a, -1, 0)
            self.send(3, 2, 0, a, -1, 0)
            self.recv((1, 0))
            self.send(1, 1, 0, 1, 1, 0)
            self.send(2, 3, 0, a, 1, 0)
            self.send(3, 3, 0, a, 1, 0)
        else:
            self.recv((2, 0))
            self.send(2, 1, 1, 0, 0, -1)
            self.send(0, 2, 1, a, 0, -1)
            self.send(1, 2, 1, a, 0, -1)
            self.recv((3, 0))
            self.send(3, 1, 1, 1, 0, 1)
            self.send(0, 3, 1, a, 0, 1)
            self.send(1, 3, 1, a, 0, 1)

    def second(self, h):
        if h == 0:
            self.recv((2, 8))
            self.send(2, 9, 0, 0, 0, -1)
            self.recv((3, 8))
            self.send(3, 9, 0, 1, 0, 1)
        else:
            self.recv((0, 8))
            self.send(0, 9, 1, 0, -1, 0)
            self.recv((1, 8))
            self.send(1, 9, 1, 1, 1, 0)

    def far(self, h):
        a = slice(None)
        if h == 0:
            self.recv((0, 1), (1, 1))
            self.send(2, 4, 0, a, 2, 0)
            self.send(3, 4, 0, a, 2, 0)
        else:
            self.recv((2, 1), (3, 1))
            self.send(0, 4, 1, a, 0, 2)
            self.send(1, 4, 1, a, 0, 2)

    def cross(self, h):
        if h == 0:
            self.recv((2, 2))
            self.send(2, 5, 0, 0, -1, -1)
            self.recv((3, 2))
            self.send(3, 5, 0, 1, -1, 1)
            self.recv((2, 3))
            self.send(2, 6, 0, 0, 1, -1)
            self.recv((3, 3))
            self.send(3, 6, 0, 1, 1, 1)
        else:
            self.recv((0, 2))
            self.send(0, 5, 1, 0, -1, -1)
            self.recv((1, 2))
            self.send(1, 5, 1, 1, 1, -1)
            self.recv((0, 3))
            self.send(0, 6, 1, 0, -1, 1)
            self.recv((1, 3))
            self.send(1, 6, 1, 1, 1, 1)

    def last(self, h):
        if h == 0:
            self.recv((2, 4))
            self.send(2, 7, 0, 0, 2, -1)
            self.recv((3, 4))
            self.send(3, 7, 0, 1, 2, 1)
        else:
            self.recv((0, 4))
            self.send(0, 7, 1, 0, -1, 2)
            self.recv((1, 4))
            self.send(1, 7, 1, 1, 1, 2)

    def drain(self):
        for c in self.copies.values():
            c.wait_send()


class GatherRep:
    def __init__(self, buf, ssem, rsem, dp, x, k):
        self.buf, self.ssem, self.rsem, self.k = buf, ssem, rsem, k
        self.x = [x, (x + 1) % 4, (x + 2) % 4, (x + 3) % 4]
        self.dev = [(dp, self.x[1] * 2 + k), (dp, self.x[3] * 2 + k), (dp, x * 2 + 1 - k)]
        self.copies = {}

    def send(self, direction, slot, u, dx):
        at = pl.ds(pl.multiple_of((self.x[dx % 4] * 2 + self.k) * CAP, CAP), CAP)
        piece = self.buf.at[u, :, at]
        c = rcopy(piece, piece, self.ssem.at[direction, slot], self.rsem.at[direction, slot], self.dev[direction])
        c.start()
        self.copies[direction, slot] = c

    def recv(self, *which):
        for w in which:
            self.copies[w].wait_recv()

    def round1(self):
        for direction in range(3):
            self.send(direction, 0, slice(None), 0)

    def round2(self):
        self.recv((0, 0))
        self.send(0, 1, 0, -1)
        self.send(2, 1, slice(None), -1)
        self.recv((1, 0))
        self.send(1, 1, 1, 1)
        self.send(2, 2, slice(None), 1)

    def round3(self):
        self.recv((0, 1))
        self.send(2, 3, 0, 2)
        self.recv((1, 1))
        self.send(2, 4, 1, 2)

    def finish(self):
        for slot in range(5):
            self.recv((2, slot))

    def drain(self):
        for c in self.copies.values():
            c.wait_send()


class ReduceRep:
    def __init__(self, full, out, sib, far, far_in, near, near_in, mid, mid_in, ssem, rsem, dp, x, k):
        self.full, self.out, self.sib = full, out, sib
        self.far, self.far_in, self.near, self.near_in, self.mid, self.mid_in = far, far_in, near, near_in, mid, mid_in
        self.ssem, self.rsem, self.k = ssem, rsem, k
        self.x = [x, (x + 1) % 4, (x + 2) % 4, (x + 3) % 4]
        self.right, self.left = (dp, self.x[1] * 2 + k), (dp, self.x[3] * 2 + k)
        self.other = (dp, x * 2 + 1 - k)
        self.copies = {}

    def send(self, kind, q, src, dst, device):
        c = rcopy(src, dst, self.ssem.at[kind, q], self.rsem.at[kind, q], device)
        c.start()
        self.copies[kind, q] = c

    def put(self, q, value):
        parts = value.reshape((4, 2) + (value.shape[0] // 8, 256))
        self.full[q] = parts
        self.out[q] = parts.astype(self.out.dtype)
        self.send(0, q, self.out.at[q, :, 1 - self.k], self.sib.at[q], self.other)

    def part(self, q, dx):
        at = self.x[dx % 4]
        return self.full[q, at, self.k] + self.sib[q, at].astype(F32)

    def step1(self, q):
        self.copies[0, q].wait_recv()
        ahead, behind = (self.right, self.left) if q < 2 else (self.left, self.right)
        self.far[q] = self.part(q, 2).astype(self.far.dtype)
        self.send(1, q, self.far.at[q], self.far_in.at[q], ahead)
        self.near[q] = self.part(q, -1 if q < 2 else 1).astype(self.near.dtype)
        self.send(2, q, self.near.at[q], self.near_in.at[q], behind)

    def step2(self, q):
        self.copies[1, q].wait_recv()
        self.mid[q] = (self.part(q, 1 if q < 2 else -1) + self.far_in[q].astype(F32)).astype(self.mid.dtype)
        self.send(3, q, self.mid.at[q], self.mid_in.at[q], self.right if q < 2 else self.left)

    def result(self, q):
        self.copies[2, q].wait_recv()
        self.copies[3, q].wait_recv()
        return self.part(q, 0) + self.near_in[q].astype(F32) + self.mid_in[q].astype(F32)

    def drain(self):
        for c in self.copies.values():
            c.wait_send()


ORDER = (0, 2, 1, 3)


def kernel(
    hidden_hbm, slot_ref, pos_ref, proj_hbm,
    pgrad_out, proj_out, loss_out,
    hid, proj, pooled, pooled_in, pooled_t, uc, ur, ec, scores, weights, rowsum, colpart, zc, zr, zl, bias_c,
    posterm, unit_s,
    g_full, g_out, g_sib, g_far, g_far_in, g_near, g_near_in, g_mid, g_mid_in,
    p_full, p_out, p_sib, p_far, p_far_in, p_near, p_near_in, p_mid, p_mid_in,
    load_sem, uc_s, uc_r, ur_s, ur_r, ec_s, ec_r, g_s, g_r, p_s, p_r, a2a_s, a2a_r, zc_s, zc_r, zr_s, zr_r, zl_s, zl_r,
):
    dp, rep = lax.axis_index("dp"), lax.axis_index("rep")
    z, y, x, k = dp // 4, dp % 4, rep // 2, rep % 2
    dp_peers = [((dp + j) % 16, rep) for j in range(1, 16)]
    rep_peers = [(dp, (rep + j) % 8) for j in range(1, 8)]

    loads = []
    for j in range(4):
        loads.append(
            (
                pltpu.make_async_copy(hidden_hbm.at[:, pl.ds(j * 1024, 1024)], hid.at[j], load_sem.at[0, j]),
                pltpu.make_async_copy(proj_hbm.at[pl.ds(j * 1024, 1024)], proj.at[pl.ds(j * 1024, 1024)], load_sem.at[1, j]),
            )
        )
        loads[-1][0].start()
        loads[-1][1].start()

    barrier = pltpu.get_barrier_semaphore()
    near = [((z + 1) % 4 * 4 + y, rep), ((z + 3) % 4 * 4 + y, rep), (z * 4 + (y + 1) % 4, rep), (z * 4 + (y + 3) % 4, rep)]
    near += [(dp, (x + 1) % 4 * 2 + k), (dp, (x + 3) % 4 * 2 + k), (dp, x * 2 + 1 - k)]
    for peer in near:
        pl.semaphore_signal(barrier, inc=1, device_id=peer, device_id_type=MESH)

    member = slot_ref[...] == lax.broadcasted_iota(jnp.int32, (CAP, TOK), 0)
    onehot = member.astype(F32)
    counts = jnp.sum(onehot, axis=1, keepdims=True)
    onehot = onehot.astype(BF16)
    denom = jnp.maximum(counts, 1.0)
    live = counts > 0.0
    embed = jnp.zeros((CAP, F), F32)
    for j in range(4):
        loads[j][0].wait()
        chunk = (jnp.dot(onehot, hid[j], preferred_element_type=F32) / denom).astype(BF16)
        for i in range(4):
            pooled[j * 4 + i] = chunk[:, i * 256 : (i + 1) * 256]
        loads[j][1].wait()
        embed = embed + jnp.dot(chunk, proj[pl.ds(j * 1024, 1024), :], preferred_element_type=F32)
    rscale = lax.rsqrt(jnp.mean(embed * embed, axis=1, keepdims=True) + 1e-06)
    unit = embed * rscale
    unit_s[...] = unit
    unit_b = unit.astype(BF16)
    lane = lax.broadcasted_iota(jnp.int32, (CAP, F), 1)
    marked = jnp.where(jnp.logical_and(lane == 0, jnp.logical_not(live)), MARK, unit).astype(BF16)
    at_c = pl.ds(pl.multiple_of(dp * CAP, CAP), CAP)
    at_r = pl.ds(pl.multiple_of(rep * CAP, CAP), CAP)
    for q in range(4):
        piece = marked[:, q * 256 : (q + 1) * 256]
        uc[q // 2, q % 2, at_c, :] = piece
        ur[q // 2, q % 2, at_r, :] = piece

    pl.semaphore_wait(barrier, 7)

    gc = GatherDp(uc, uc_s, uc_r, z, y, rep)
    gr = GatherRep(ur, ur_s, ur_r, dp, x, k)
    gc.start(0)
    gc.start(1)
    gr.round1()

    at_pos = pos_ref[...] - (dp * 8 + rep) * CAP
    row80 = lax.broadcasted_iota(jnp.int32, (CAP, CAP), 0)
    col80 = lax.broadcasted_iota(jnp.int32, (CAP, CAP), 1)
    back = jnp.where(jnp.logical_and(at_pos == row80, row80 != col80), 1.0, 0.0).astype(BF16)
    partner = lax.dot_general(back, unit_b, (((0,), (0,)), ((), ())), preferred_element_type=F32)
    posterm[...] = partner + jnp.dot(back, unit_b, preferred_element_type=F32)
    picked = jnp.sum(jnp.sum(partner * unit_b.astype(F32), axis=1, keepdims=True), axis=0, keepdims=True) * MULT

    def pair_sums(blocks, own):
        cols = jnp.concatenate(
            [jnp.concatenate([uc[q // 2, q % 2, gc.at(*b), :] for q in range(4)], axis=1) for b in blocks], axis=0
        )
        bias = jnp.where(cols[:, 0:1].astype(F32) < 128.0, 0.0, NEG)
        s = lax.dot_general(cols, rows, (((1,), (1,)), ((), ())), preferred_element_type=F32) * (MULT * LOG2E)
        s = s + bias + bias_l
        if own:
            lane = lax.broadcasted_iota(jnp.int32, (CAP, ROWS), 1) - rep * CAP
            s = jnp.where(lane == lax.broadcasted_iota(jnp.int32, (CAP, ROWS), 0), NEG, s)
        e = jnp.exp2(s)
        part = e[:, :128]
        for i in range(1, 5):
            part = part + e[:, i * 128 : (i + 1) * 128]
        for i, b in enumerate(blocks):
            colpart[gc.at(*b), :] = part[i * CAP : (i + 1) * CAP]
        return jnp.sum(e, axis=0, keepdims=True)

    gc.first(0)
    gc.first(1)
    gr.round2()
    gc.far(0)
    gc.far(1)
    gr.round3()
    gc.second(0)
    gc.second(1)
    gr.finish()
    rows = jnp.concatenate([ur[q // 2, q % 2] for q in range(4)], axis=1)
    live_r = ur[0, 0, :, 0:1].astype(F32) < 128.0
    bias_r = jnp.where(live_r, 0.0, NEG)
    pick0 = jnp.where(lax.broadcasted_iota(jnp.int32, (16, 256), 1) == 0, 1.0, 0.0).astype(BF16)
    first = lax.dot_general(pick0, ur[0, 0], (((1,), (1,)), ((), ())), preferred_element_type=F32)
    bias_l = jnp.where(first[0:1] < 128.0, 0.0, NEG)
    nlive_r = jnp.sum(jnp.where(bias_l < -1.0, 0.0, 1.0), axis=1, keepdims=True)
    sum_r = pair_sums([(0, 0)], True)
    gc.cross(0)
    gc.cross(1)
    gc.last(0)
    gc.last(1)
    sum_r = sum_r + pair_sums([(-1, 0), (1, 0), (0, -1), (0, 1)], False)
    for direction in range(4):
        gc.recv((direction, 9))
    sum_r = sum_r + pair_sums([(-1, -1), (-1, 1), (1, -1), (1, 1), (2, 0), (0, 2)], False)
    for slot in (5, 6):
        for direction in range(4):
            gc.recv((direction, slot))
    sum_r = sum_r + pair_sums([(-1, 2), (1, 2), (2, -1), (2, 1)], False)
    for direction in range(4):
        gc.recv((direction, 7))
    sum_r = sum_r + pair_sums([(2, 2)], False)
    zr[rep] = sum_r
    zc[dp, :, pl.ds(0, COLS)] = jnp.sum(colpart[...].T, axis=0, keepdims=True)
    l128 = lax.broadcasted_iota(jnp.int32, (1, 128), 1)
    zc[dp, :, pl.ds(COLS, 128)] = jnp.where(l128 == 0, nlive_r, jnp.where(l128 == 1, picked, 0.0))

    zcopies = []
    for j in range(15):
        zcopies.append(rcopy(zc.at[dp], zc.at[dp], zc_s.at[j], zc_r.at[j], dp_peers[j]))
        zcopies[-1].start()
    for j in range(7):
        zcopies.append(rcopy(zr.at[rep], zr.at[rep], zr_s.at[j], zr_r.at[j], rep_peers[j]))
        zcopies[-1].start()

    a2a = []
    for j in range(15):
        peer = dp_peers[j]
        c = rcopy(pooled.at[peer[0]], pooled_in.at[at_c], a2a_s.at[j], a2a_r.at[j], peer)
        c.start()
        a2a.append(c)
    pooled_in[at_c, :] = pooled[dp]

    id_r = lax.broadcasted_iota(jnp.int32, (ROWS, 1), 0) - rep * CAP
    id_r = jnp.where(jnp.logical_and(id_r >= 0, id_r < CAP), id_r, -1)

    def score_tile(t, carry):
        at = pl.ds(pl.multiple_of(t * 256, 256), 256)
        cols = jnp.concatenate([uc[q // 2, q % 2, at, :] for q in range(4)], axis=1)
        first = lax.dot_general(pick0, cols[:, :256], (((1,), (1,)), ((), ())), preferred_element_type=F32)
        bias = jnp.where(first[0:1] < 128.0, 0.0, NEG)
        bias_c[:, at] = bias
        id_c = lax.broadcasted_iota(jnp.int32, (1, 256), 1) + t * 256 - dp * CAP
        id_c = jnp.where(jnp.logical_and(id_c >= 0, id_c < CAP), id_c, -2)
        s = lax.dot_general(rows, cols, (((1,), (1,)), ((), ())), preferred_element_type=F32) * (MULT * LOG2E)
        scores[:, at] = jnp.where(id_r == id_c, NEG, s + bias_r + bias)
        return carry

    lax.fori_loop(0, 5, score_tile, 0)
    for c in zcopies:
        c.wait_recv()

    total_c = zc[0]
    for j in range(1, 16):
        total_c = total_c + zc[j]
    total_r = zr[0]
    for j in range(1, 8):
        total_r = total_r + zr[j]
    nlive = total_c[:, COLS : COLS + 1]
    log_c = jnp.where(bias_c[...] < -1.0, 0.0, jnp.log(total_c[:, :COLS]))
    loss_c = jnp.sum(log_c, axis=1, keepdims=True) - total_c[:, COLS + 1 : COLS + 2]
    zl[rep] = jnp.broadcast_to(loss_c, (1, 128))
    lcopies = []
    for j in range(7):
        lcopies.append(rcopy(zl.at[rep], zl.at[rep], zl_s.at[j], zl_r.at[j], rep_peers[j]))
        lcopies[-1].start()
    bias_c[...] = log_c * LOG2E
    log_r = jnp.broadcast_to(jnp.log(total_r) * LOG2E, (128, ROWS)).T
    log_r = jnp.where(live_r, log_r, 0.0)
    rowsum[...] = log_r

    def weight_tile(t, carry):
        at = pl.ds(pl.multiple_of(t * 128, 128), 128)
        s = scores[:, at]
        w = jnp.exp2(s - rowsum[...]) + jnp.exp2(s - bias_c[:, at])
        weights[:, at] = w.astype(BF16)
        return carry

    lax.fori_loop(0, 10, weight_tile, 0)

    red = ReduceRep(g_full, g_out, g_sib, g_far, g_far_in, g_near, g_near_in, g_mid, g_mid_in, g_s, g_r, dp, x, k)
    for q in ORDER:
        red.put(q, jnp.dot(weights[...], uc[q // 2, q % 2], preferred_element_type=F32))
    for q in ORDER:
        red.step1(q)
    for q in ORDER:
        red.step2(q)
    got = jnp.concatenate([red.result(q) for q in range(4)], axis=1)
    unit = unit_s[...]
    ugrad = (got - posterm[...]) * (MULT / nlive)
    inner = jnp.mean(unit * ugrad, axis=1, keepdims=True)
    egrad = (rscale * (ugrad - unit * inner)).astype(BF16)
    for q in range(4):
        ec[q // 2, q % 2, at_c, :] = egrad[:, q * 256 : (q + 1) * 256]

    ge = GatherDp(ec, ec_s, ec_r, z, y, rep)

    def pgrad(j):
        at = pl.ds(j * 512, 512)
        part = lax.dot_general(egrad, proj[at, :], (((1,), (1,)), ((), ())), preferred_element_type=F32)
        pgrad_out[:, at] = (part / denom).astype(BF16)

    ge.start(0)
    ge.start(1)
    for c in a2a:
        c.wait_recv()
    pooled_t[...] = pooled_in[...].astype(F32).T.astype(BF16)
    ge.first(0)
    ge.first(1)
    pgrad(0)
    ge.far(0)
    ge.far(1)
    ge.second(0)
    ge.second(1)
    pgrad(1)
    pgrad(2)
    ge.cross(0)
    ge.cross(1)
    pgrad(3)
    ge.last(0)
    ge.last(1)
    for j in range(4, 8):
        pgrad(j)
    for slot in (9, 5, 6, 7):
        for direction in range(4):
            ge.recv((direction, slot))

    red2 = ReduceRep(p_full, p_out, p_sib, p_far, p_far_in, p_near, p_near_in, p_mid, p_mid_in, p_s, p_r, dp, x, k)
    for q in ORDER:
        red2.put(q, jnp.dot(pooled_t[...], ec[q // 2, q % 2], preferred_element_type=F32))
    for q in ORDER:
        red2.step1(q)
    for q in ORDER:
        red2.step2(q)
    for q in range(4):
        proj_out[:, q * 256 : (q + 1) * 256] = red2.result(q)

    for c in lcopies:
        c.wait_recv()
    loss = zl[0]
    for j in range(1, 8):
        loss = loss + zl[j]
    loss_out[...] = loss / nlive

    for group in (gc, gr, red, ge, red2):
        group.drain()
    for c in a2a + zcopies + lcopies:
        c.wait_send()


def reduce_scratch(n, kind):
    return [pltpu.VMEM((4, 4, 2, n, 256), F32), pltpu.VMEM((4, 4, 2, n, 256), kind), pltpu.VMEM((4, 4, n, 256), kind)] + [
        pltpu.VMEM((4, n, 256), kind) for _ in range(6)
    ]


def local(hidden, step_slot, positive, proj):
    dma = pltpu.SemaphoreType.DMA
    vm = pl.BlockSpec(memory_space=pltpu.VMEM)
    hbm = pl.BlockSpec(memory_space=pl.ANY)
    pooled_grad, proj_grad, loss = pl.pallas_call(
        kernel,
        out_shape=(
            jax.ShapeDtypeStruct((CAP, D), BF16),
            jax.ShapeDtypeStruct((32, F), F32),
            jax.ShapeDtypeStruct((1, 128), F32),
        ),
        in_specs=[hbm, vm, vm, hbm],
        out_specs=(vm, vm, vm),
        scratch_shapes=[
            pltpu.VMEM((4, TOK, 1024), BF16),
            pltpu.VMEM((D, F), BF16),
            pltpu.VMEM((16, CAP, 256), BF16),
            pltpu.VMEM((COLS, 256), BF16),
            pltpu.VMEM((256, COLS), BF16),
            pltpu.VMEM((2, 2, COLS, 256), BF16),
            pltpu.VMEM((2, 2, ROWS, 256), BF16),
            pltpu.VMEM((2, 2, COLS, 256), BF16),
            pltpu.VMEM((ROWS, COLS), F32),
            pltpu.VMEM((ROWS, COLS), BF16),
            pltpu.VMEM((ROWS, 128), F32),
            pltpu.VMEM((COLS, 128), F32),
            pltpu.VMEM((16, 1, EXTRA), F32),
            pltpu.VMEM((8, 1, ROWS), F32),
            pltpu.VMEM((8, 1, 128), F32),
            pltpu.VMEM((1, COLS), F32),
            pltpu.VMEM((CAP, F), F32),
            pltpu.VMEM((CAP, F), F32),
        ]
        + reduce_scratch(CAP, BF16)
        + reduce_scratch(32, BF16)
        + [
            dma((2, 4)),
            dma((4, 10)), dma((4, 10)), dma((3, 5)), dma((3, 5)), dma((4, 10)), dma((4, 10)),
            dma((4, 4)), dma((4, 4)), dma((4, 4)), dma((4, 4)),
            dma((15,)), dma((15,)), dma((15,)), dma((15,)), dma((7,)), dma((7,)), dma((7,)), dma((7,)),
        ],
        compiler_params=pltpu.CompilerParams(
            collective_id=0, has_side_effects=True, vmem_limit_bytes=60 * 1024 * 1024
        ),
        cost_estimate=pl.CostEstimate(flops=6_000_000_000, bytes_accessed=14_000_000, transcendentals=2_000_000),
    )(hidden, step_slot.reshape(1, TOK), positive.reshape(1, CAP), proj)
    onehot = (step_slot[None, :] == lax.broadcasted_iota(jnp.int32, (CAP, TOK), 0)).astype(BF16)
    hidden_grad = lax.dot_general(onehot, pooled_grad, (((0,), (0,)), ((), ())), preferred_element_type=F32)
    return (hidden_grad.astype(BF16), proj_grad, loss[0, 0])


def solution(mesh):
    in_specs = (P(("dp", "rep"), None), P(("dp", "rep")), P(("dp", "rep")), P())
    out_specs = (P(("dp", "rep"), None), P(("dp", "rep"), None), P())
    return jax.shard_map(local, mesh=mesh, in_specs=in_specs, out_specs=out_specs, check_vma=False)
```

```python
import functools
import math

import jax
import jax.numpy as jnp
from jax import lax
from jax.experimental import pallas as pl
from jax.experimental.pallas import tpu as pltpu
from jax.sharding import PartitionSpec as P

MESH = pl.DeviceIdType.MESH
F32 = jnp.float32
BF16 = jnp.bfloat16
CAP = 80
TOK = 384
D = 4096
F = 1024
ROWS = 640
COLS = 1280
EXTRA = COLS + 128
MULT = 1.0 / (0.3 * math.sqrt(F))
LOG2E = 1.4426950408889634
NEG = -1e30
MARK = 256.0


def rcopy(src, dst, send_sem, recv_sem, device):
    return pltpu.make_async_remote_copy(
        src_ref=src, dst_ref=dst, send_sem=send_sem, recv_sem=recv_sem, device_id=device, device_id_type=MESH
    )


class GatherDp:
    def __init__(self, buf, ssem, rsem, z, y, rep):
        self.buf, self.ssem, self.rsem = buf, ssem, rsem
        self.z = [z, (z + 1) % 4, (z + 2) % 4, (z + 3) % 4]
        self.y = [y, (y + 1) % 4, (y + 2) % 4, (y + 3) % 4]
        self.dev = [
            (self.z[1] * 4 + y, rep),
            (self.z[3] * 4 + y, rep),
            (z * 4 + self.y[1], rep),
            (z * 4 + self.y[3], rep),
        ]
        self.copies = {}

    def at(self, dz, dy):
        return pl.ds(pl.multiple_of((self.z[dz % 4] * 4 + self.y[dy % 4]) * CAP, CAP), CAP)

    def send(self, direction, slot, h, d, dz, dy):
        piece = self.buf.at[h, d, self.at(dz, dy)]
        c = rcopy(piece, piece, self.ssem.at[direction, slot], self.rsem.at[direction, slot], self.dev[direction])
        c.start()
        self.copies[direction, slot] = c

    def recv(self, *which):
        for w in which:
            self.copies[w].wait_recv()

    def start(self, h):
        a = slice(None)
        for direction in (0, 1) if h == 0 else (2, 3):
            self.send(direction, 0, h, a, 0, 0)
        for direction in (2, 3) if h == 0 else (0, 1):
            self.send(direction, 8, h, a, 0, 0)

    def first(self, h):
        a = slice(None)
        if h == 0:
            self.recv((0, 0))
            self.send(0, 1, 0, 0, -1, 0)
            self.send(2, 2, 0, a, -1, 0)
            self.send(3, 2, 0, a, -1, 0)
            self.recv((1, 0))
            self.send(1, 1, 0, 1, 1, 0)
            self.send(2, 3, 0, a, 1, 0)
            self.send(3, 3, 0, a, 1, 0)
        else:
            self.recv((2, 0))
            self.send(2, 1, 1, 0, 0, -1)
            self.send(0, 2, 1, a, 0, -1)
            self.send(1, 2, 1, a, 0, -1)
            self.recv((3, 0))
            self.send(3, 1, 1, 1, 0, 1)
            self.send(0, 3, 1, a, 0, 1)
            self.send(1, 3, 1, a, 0, 1)

    def second(self, h):
        if h == 0:
            self.recv((2, 8))
            self.send(2, 9, 0, 0, 0, -1)
            self.recv((3, 8))
            self.send(3, 9, 0, 1, 0, 1)
        else:
            self.recv((0, 8))
            self.send(0, 9, 1, 0, -1, 0)
            self.recv((1, 8))
            self.send(1, 9, 1, 1, 1, 0)

    def far(self, h):
        a = slice(None)
        if h == 0:
            self.recv((0, 1), (1, 1))
            self.send(2, 4, 0, a, 2, 0)
            self.send(3, 4, 0, a, 2, 0)
        else:
            self.recv((2, 1), (3, 1))
            self.send(0, 4, 1, a, 0, 2)
            self.send(1, 4, 1, a, 0, 2)

    def cross(self, h):
        if h == 0:
            self.recv((2, 2))
            self.send(2, 5, 0, 0, -1, -1)
            self.recv((3, 2))
            self.send(3, 5, 0, 1, -1, 1)
            self.recv((2, 3))
            self.send(2, 6, 0, 0, 1, -1)
            self.recv((3, 3))
            self.send(3, 6, 0, 1, 1, 1)
        else:
            self.recv((0, 2))
            self.send(0, 5, 1, 0, -1, -1)
            self.recv((1, 2))
            self.send(1, 5, 1, 1, 1, -1)
            self.recv((0, 3))
            self.send(0, 6, 1, 0, -1, 1)
            self.recv((1, 3))
            self.send(1, 6, 1, 1, 1, 1)

    def last(self, h):
        if h == 0:
            self.recv((2, 4))
            self.send(2, 7, 0, 0, 2, -1)
            self.recv((3, 4))
            self.send(3, 7, 0, 1, 2, 1)
        else:
            self.recv((0, 4))
            self.send(0, 7, 1, 0, -1, 2)
            self.recv((1, 4))
            self.send(1, 7, 1, 1, 1, 2)

    def drain(self):
        for c in self.copies.values():
            c.wait_send()


class GatherRep:
    def __init__(self, buf, ssem, rsem, dp, x, k):
        self.buf, self.ssem, self.rsem, self.k = buf, ssem, rsem, k
        self.x = [x, (x + 1) % 4, (x + 2) % 4, (x + 3) % 4]
        self.dev = [(dp, self.x[1] * 2 + k), (dp, self.x[3] * 2 + k), (dp, x * 2 + 1 - k)]
        self.copies = {}

    def send(self, direction, slot, u, dx):
        at = pl.ds(pl.multiple_of((self.x[dx % 4] * 2 + self.k) * CAP, CAP), CAP)
        piece = self.buf.at[u, :, at]
        c = rcopy(piece, piece, self.ssem.at[direction, slot], self.rsem.at[direction, slot], self.dev[direction])
        c.start()
        self.copies[direction, slot] = c

    def recv(self, *which):
        for w in which:
            self.copies[w].wait_recv()

    def round1(self):
        self.send(0, 0, 0, 0)
        self.send(1, 0, 1, 0)
        self.send(0, 2, 1, 0)
        self.send(1, 2, 0, 0)
        self.send(2, 0, slice(None), 0)

    def round2(self):
        self.recv((0, 0))
        self.send(0, 1, 0, -1)
        self.send(2, 1, 0, -1)
        self.recv((1, 0))
        self.send(1, 1, 1, 1)
        self.send(2, 2, 1, 1)

    def round3(self):
        self.recv((0, 2))
        self.send(2, 3, 1, -1)
        self.recv((1, 2))
        self.send(2, 4, 0, 1)

    def round4(self):
        self.recv((0, 1))
        self.send(2, 5, 0, 2)
        self.recv((1, 1))
        self.send(2, 6, 1, 2)

    def finish(self):
        for slot in range(7):
            self.recv((2, slot))

    def drain(self):
        for c in self.copies.values():
            c.wait_send()


class ReduceRep:
    def __init__(self, full, out, sib, far, far_in, near, near_in, mid, mid_in, ssem, rsem, dp, x, k):
        self.full, self.out, self.sib = full, out, sib
        self.far, self.far_in, self.near, self.near_in, self.mid, self.mid_in = far, far_in, near, near_in, mid, mid_in
        self.ssem, self.rsem, self.k = ssem, rsem, k
        self.x = [x, (x + 1) % 4, (x + 2) % 4, (x + 3) % 4]
        self.right, self.left = (dp, self.x[1] * 2 + k), (dp, self.x[3] * 2 + k)
        self.other = (dp, x * 2 + 1 - k)
        self.copies = {}

    def send(self, kind, q, src, dst, device):
        c = rcopy(src, dst, self.ssem.at[kind, q], self.rsem.at[kind, q], device)
        c.start()
        self.copies[kind, q] = c

    def put(self, q, value):
        parts = value.reshape((4, 2) + (value.shape[0] // 8, 256))
        self.full[q] = parts
        self.out[q] = parts.astype(self.out.dtype)
        self.send(0, q, self.out.at[q, :, 1 - self.k], self.sib.at[q], self.other)

    def part(self, q, dx):
        at = self.x[dx % 4]
        return self.full[q, at, self.k] + self.sib[q, at].astype(F32)

    def step1(self, q):
        self.copies[0, q].wait_recv()
        ahead, behind = (self.right, self.left) if q < 2 else (self.left, self.right)
        self.far[q] = self.part(q, 2).astype(self.far.dtype)
        self.send(1, q, self.far.at[q], self.far_in.at[q], ahead)
        self.near[q] = self.part(q, -1 if q < 2 else 1).astype(self.near.dtype)
        self.send(2, q, self.near.at[q], self.near_in.at[q], behind)

    def step2(self, q):
        self.copies[1, q].wait_recv()
        self.mid[q] = (self.part(q, 1 if q < 2 else -1) + self.far_in[q].astype(F32)).astype(self.mid.dtype)
        self.send(3, q, self.mid.at[q], self.mid_in.at[q], self.right if q < 2 else self.left)

    def result(self, q):
        self.copies[2, q].wait_recv()
        self.copies[3, q].wait_recv()
        return self.part(q, 0) + self.near_in[q].astype(F32) + self.mid_in[q].astype(F32)

    def drain(self):
        for c in self.copies.values():
            c.wait_send()


ORDER = (0, 2, 1, 3)


def kernel(
    hidden_hbm, slot_ref, pos_ref, proj_hbm,
    pgrad_out, proj_out, loss_out,
    hid, proj, pooled, pooled_in, uc, ur, ec, scores, weights, rowsum, colpart, zc, zr, zl, bias_c,
    posterm, unit_s,
    g_full, g_out, g_sib, g_far, g_far_in, g_near, g_near_in, g_mid, g_mid_in,
    p_full, p_out, p_sib, p_send, p_in,
    load_sem, uc_s, uc_r, ur_s, ur_r, ec_s, ec_r, g_s, g_r, p_s, p_r, a2a_s, a2a_r, zc_s, zc_r, zr_s, zr_r, zl_s, zl_r,
):
    dp, rep = lax.axis_index("dp"), lax.axis_index("rep")
    z, y, x, k = dp // 4, dp % 4, rep // 2, rep % 2
    dp_peers = [((dp + j) % 16, rep) for j in range(1, 16)]
    rep_peers = [(dp, (rep + j) % 8) for j in range(1, 8)]

    loads = []
    for j in range(4):
        loads.append(
            (
                pltpu.make_async_copy(hidden_hbm.at[:, pl.ds(j * 1024, 1024)], hid.at[j], load_sem.at[0, j]),
                pltpu.make_async_copy(proj_hbm.at[pl.ds(j * 1024, 1024)], proj.at[pl.ds(j * 1024, 1024)], load_sem.at[1, j]),
            )
        )
        loads[-1][0].start()
        loads[-1][1].start()

    barrier = pltpu.get_barrier_semaphore()
    near = [((z + 1) % 4 * 4 + y, rep), ((z + 3) % 4 * 4 + y, rep), (z * 4 + (y + 1) % 4, rep), (z * 4 + (y + 3) % 4, rep)]
    near += [(dp, (x + 1) % 4 * 2 + k), (dp, (x + 3) % 4 * 2 + k), (dp, x * 2 + 1 - k)]
    for peer in near:
        pl.semaphore_signal(barrier, inc=1, device_id=peer, device_id_type=MESH)

    member = slot_ref[...] == lax.broadcasted_iota(jnp.int32, (CAP, TOK), 0)
    onehot = member.astype(F32)
    counts = jnp.sum(onehot, axis=1, keepdims=True)
    onehot = onehot.astype(BF16)
    denom = jnp.maximum(counts, 1.0)
    live = counts > 0.0
    embed = jnp.zeros((CAP, F), F32)
    for j in range(4):
        loads[j][0].wait()
        chunk = (jnp.dot(onehot, hid[j], preferred_element_type=F32) / denom).astype(BF16)
        for i in range(4):
            pooled[j * 4 + i] = chunk[:, i * 256 : (i + 1) * 256]
        loads[j][1].wait()
        embed = embed + jnp.dot(chunk, proj[pl.ds(j * 1024, 1024), :], preferred_element_type=F32)
    rscale = lax.rsqrt(jnp.mean(embed * embed, axis=1, keepdims=True) + 1e-06)
    unit = embed * rscale
    unit_s[...] = unit
    unit_b = unit.astype(BF16)
    lane = lax.broadcasted_iota(jnp.int32, (CAP, F), 1)
    marked = jnp.where(jnp.logical_and(lane == 0, jnp.logical_not(live)), MARK, unit).astype(BF16)
    at_c = pl.ds(pl.multiple_of(dp * CAP, CAP), CAP)
    at_r = pl.ds(pl.multiple_of(rep * CAP, CAP), CAP)
    for q in range(4):
        piece = marked[:, q * 256 : (q + 1) * 256]
        uc[q // 2, q % 2, at_c, :] = piece
        ur[q // 2, q % 2, at_r, :] = piece

    pl.semaphore_wait(barrier, 7)

    gc = GatherDp(uc, uc_s, uc_r, z, y, rep)
    gr = GatherRep(ur, ur_s, ur_r, dp, x, k)
    gc.start(0)
    gc.start(1)
    gr.round1()

    at_pos = pos_ref[...] - (dp * 8 + rep) * CAP
    row80 = lax.broadcasted_iota(jnp.int32, (CAP, CAP), 0)
    col80 = lax.broadcasted_iota(jnp.int32, (CAP, CAP), 1)
    back = jnp.where(jnp.logical_and(at_pos == row80, row80 != col80), 1.0, 0.0).astype(BF16)
    partner = lax.dot_general(back, unit_b, (((0,), (0,)), ((), ())), preferred_element_type=F32)
    posterm[...] = partner + jnp.dot(back, unit_b, preferred_element_type=F32)
    picked = jnp.sum(jnp.sum(partner * unit_b.astype(F32), axis=1, keepdims=True), axis=0, keepdims=True) * MULT

    def pair_sums(blocks, own):
        cols = jnp.concatenate(
            [jnp.concatenate([uc[q // 2, q % 2, gc.at(*b), :] for q in range(4)], axis=1) for b in blocks], axis=0
        )
        bias = jnp.where(cols[:, 0:1].astype(F32) < 128.0, 0.0, NEG)
        s = lax.dot_general(cols, rows, (((1,), (1,)), ((), ())), preferred_element_type=F32) * (MULT * LOG2E)
        s = s + bias + bias_l
        if own:
            lane = lax.broadcasted_iota(jnp.int32, (CAP, ROWS), 1) - rep * CAP
            s = jnp.where(lane == lax.broadcasted_iota(jnp.int32, (CAP, ROWS), 0), NEG, s)
        e = jnp.exp2(s)
        part = e[:, :128]
        for i in range(1, 5):
            part = part + e[:, i * 128 : (i + 1) * 128]
        for i, b in enumerate(blocks):
            colpart[gc.at(*b), :] = part[i * CAP : (i + 1) * CAP]
        return jnp.sum(e, axis=0, keepdims=True)

    gc.first(0)
    gc.first(1)
    gr.round2()
    gc.far(0)
    gc.far(1)
    gr.round3()
    gc.second(0)
    gc.second(1)
    gr.round4()
    gc.cross(0)
    gc.cross(1)
    gr.finish()
    rows = jnp.concatenate([ur[q // 2, q % 2] for q in range(4)], axis=1)
    live_r = ur[0, 0, :, 0:1].astype(F32) < 128.0
    bias_r = jnp.where(live_r, 0.0, NEG)
    pick0 = jnp.where(lax.broadcasted_iota(jnp.int32, (16, 256), 1) == 0, 1.0, 0.0).astype(BF16)
    first = lax.dot_general(pick0, ur[0, 0], (((1,), (1,)), ((), ())), preferred_element_type=F32)
    bias_l = jnp.where(first[0:1] < 128.0, 0.0, NEG)
    nlive_r = jnp.sum(jnp.where(bias_l < -1.0, 0.0, 1.0), axis=1, keepdims=True)
    sum_r = pair_sums([(0, 0)], True)
    gc.last(0)
    gc.last(1)
    sum_r = sum_r + pair_sums([(-1, 0), (1, 0), (0, -1), (0, 1)], False)
    for direction in range(4):
        gc.recv((direction, 9))
    sum_r = sum_r + pair_sums([(-1, -1), (-1, 1), (1, -1), (1, 1), (2, 0), (0, 2)], False)
    for slot in (5, 6):
        for direction in range(4):
            gc.recv((direction, slot))
    sum_r = sum_r + pair_sums([(-1, 2), (1, 2), (2, -1), (2, 1)], False)
    for direction in range(4):
        gc.recv((direction, 7))
    sum_r = sum_r + pair_sums([(2, 2)], False)
    zr[rep] = sum_r
    zc[dp, :, pl.ds(0, COLS)] = jnp.sum(colpart[...].T, axis=0, keepdims=True)
    l128 = lax.broadcasted_iota(jnp.int32, (1, 128), 1)
    zc[dp, :, pl.ds(COLS, 128)] = jnp.where(l128 == 0, nlive_r, jnp.where(l128 == 1, picked, 0.0))

    zcopies = []
    for j in range(15):
        zcopies.append(rcopy(zc.at[dp], zc.at[dp], zc_s.at[j], zc_r.at[j], dp_peers[j]))
        zcopies[-1].start()
    for j in range(7):
        zcopies.append(rcopy(zr.at[rep], zr.at[rep], zr_s.at[j], zr_r.at[j], rep_peers[j]))
        zcopies[-1].start()

    id_r = lax.broadcasted_iota(jnp.int32, (ROWS, 1), 0) - rep * CAP
    id_r = jnp.where(jnp.logical_and(id_r >= 0, id_r < CAP), id_r, -1)

    def score_tile(t, carry):
        at = pl.ds(pl.multiple_of(t * 256, 256), 256)
        cols = jnp.concatenate([uc[q // 2, q % 2, at, :] for q in range(4)], axis=1)
        first = lax.dot_general(pick0, cols[:, :256], (((1,), (1,)), ((), ())), preferred_element_type=F32)
        bias = jnp.where(first[0:1] < 128.0, 0.0, NEG)
        bias_c[:, at] = bias
        id_c = lax.broadcasted_iota(jnp.int32, (1, 256), 1) + t * 256 - dp * CAP
        id_c = jnp.where(jnp.logical_and(id_c >= 0, id_c < CAP), id_c, -2)
        s = lax.dot_general(rows, cols, (((1,), (1,)), ((), ())), preferred_element_type=F32) * (MULT * LOG2E)
        scores[:, at] = jnp.where(id_r == id_c, NEG, s + bias_r + bias)
        return carry

    lax.fori_loop(0, 5, score_tile, 0)
    for c in zcopies:
        c.wait_recv()

    total_c = zc[0]
    for j in range(1, 16):
        total_c = total_c + zc[j]
    total_r = zr[0]
    for j in range(1, 8):
        total_r = total_r + zr[j]
    nlive = total_c[:, COLS : COLS + 1]
    log_c = jnp.where(bias_c[...] < -1.0, 0.0, jnp.log(total_c[:, :COLS]))
    bias_c[...] = log_c * LOG2E
    log_r = jnp.broadcast_to(jnp.log(total_r) * LOG2E, (128, ROWS)).T
    log_r = jnp.where(live_r, log_r, 0.0)
    rowsum[...] = log_r

    def weight_tile(t, carry):
        at = pl.ds(pl.multiple_of(t * 128, 128), 128)
        s = scores[:, at]
        w = jnp.exp2(s - rowsum[...]) + jnp.exp2(s - bias_c[:, at])
        weights[:, at] = w.astype(BF16)
        return carry

    lax.fori_loop(0, 10, weight_tile, 0)

    red = ReduceRep(g_full, g_out, g_sib, g_far, g_far_in, g_near, g_near_in, g_mid, g_mid_in, g_s, g_r, dp, x, k)
    for q in ORDER:
        red.put(q, jnp.dot(weights[...], uc[q // 2, q % 2], preferred_element_type=F32))
    for q in ORDER:
        red.step1(q)
    a2a = []
    for j in range(15):
        peer = dp_peers[j]
        c = rcopy(pooled.at[peer[0]], pooled_in.at[at_c], a2a_s.at[j], a2a_r.at[j], peer)
        c.start()
        a2a.append(c)
    pooled_in[at_c, :] = pooled[dp]

    for q in ORDER:
        red.step2(q)
    loss_c = jnp.sum(log_c, axis=1, keepdims=True) - total_c[:, COLS + 1 : COLS + 2]
    zl[rep] = jnp.broadcast_to(loss_c, (1, 128))
    lcopies = []
    for j in range(7):
        lcopies.append(rcopy(zl.at[rep], zl.at[rep], zl_s.at[j], zl_r.at[j], rep_peers[j]))
        lcopies[-1].start()
    got = jnp.concatenate([red.result(q) for q in range(4)], axis=1)
    unit = unit_s[...]
    ugrad = (got - posterm[...]) * (MULT / nlive)
    inner = jnp.mean(unit * ugrad, axis=1, keepdims=True)
    egrad = (rscale * (ugrad - unit * inner)).astype(BF16)
    for q in range(4):
        ec[q // 2, q % 2, at_c, :] = egrad[:, q * 256 : (q + 1) * 256]

    ge = GatherDp(ec, ec_s, ec_r, z, y, rep)

    def pgrad(j):
        at = pl.ds(j * 512, 512)
        part = lax.dot_general(egrad, proj[at, :], (((1,), (1,)), ((), ())), preferred_element_type=F32)
        pgrad_out[:, at] = (part / denom).astype(BF16)

    def proj_part(blocks, begin=False):
        left = jnp.concatenate([pooled_in[ge.at(*b), :] for b in blocks], axis=0).astype(F32).T.astype(BF16)
        for q in range(4):
            right = jnp.concatenate([ec[q // 2, q % 2, ge.at(*b), :] for b in blocks], axis=0)
            part = jnp.dot(left, right, preferred_element_type=F32).reshape(4, 2, 32, 256)
            p_full[q] = part if begin else p_full[q] + part

    ge.start(0)
    ge.start(1)
    for c in a2a:
        c.wait_recv()
    proj_part([(0, 0)], True)
    ge.first(0)
    ge.first(1)
    pgrad(0)
    ge.far(0)
    ge.far(1)
    ge.second(0)
    ge.second(1)
    pgrad(1)
    pgrad(2)
    ge.cross(0)
    ge.cross(1)
    pgrad(3)
    ge.last(0)
    ge.last(1)
    for j in range(4, 8):
        pgrad(j)
    proj_part([(-1, 0), (1, 0), (0, -1), (0, 1)])
    for direction in range(4):
        ge.recv((direction, 9))
    proj_part([(-1, -1), (-1, 1), (1, -1), (1, 1), (2, 0), (0, 2)])
    for slot in (5, 6):
        for direction in range(4):
            ge.recv((direction, slot))
    proj_part([(-1, 2), (1, 2), (2, -1), (2, 1)])
    for direction in range(4):
        ge.recv((direction, 7))
    proj_part([(2, 2)])

    p_out[...] = p_full[:, :, 1 - k].astype(BF16)
    pcopy = rcopy(p_out, p_sib, p_s.at[3], p_r.at[3], (dp, x * 2 + 1 - k))
    pcopy.start()
    pcopy.wait_recv()
    pcopies = [pcopy]
    for j in range(1, 4):
        to = (x + j) % 4
        p_send[j - 1] = (p_full[:, to, k] + p_sib[:, to].astype(F32)).astype(BF16)
        c = rcopy(p_send.at[j - 1], p_in.at[j - 1], p_s.at[j - 1], p_r.at[j - 1], (dp, to * 2 + k))
        c.start()
        pcopies.append(c)
    total = p_full[:, x, k] + p_sib[:, x].astype(F32)
    for c in pcopies[1:]:
        c.wait_recv()
    total = total + p_in[0].astype(F32) + p_in[1].astype(F32) + p_in[2].astype(F32)
    for q in range(4):
        proj_out[:, q * 256 : (q + 1) * 256] = total[q]

    for c in lcopies:
        c.wait_recv()
    loss = zl[0]
    for j in range(1, 8):
        loss = loss + zl[j]
    loss_out[...] = loss / nlive

    for group in (gc, gr, red, ge):
        group.drain()
    for c in a2a + zcopies + lcopies + pcopies:
        c.wait_send()


def reduce_scratch(n, kind):
    return [pltpu.VMEM((4, 4, 2, n, 256), F32), pltpu.VMEM((4, 4, 2, n, 256), kind), pltpu.VMEM((4, 4, n, 256), kind)] + [
        pltpu.VMEM((4, n, 256), kind) for _ in range(6)
    ]


def local(hidden, step_slot, positive, proj):
    dma = pltpu.SemaphoreType.DMA
    slots = step_slot.reshape(1, TOK)
    vm = pl.BlockSpec(memory_space=pltpu.VMEM)
    hbm = pl.BlockSpec(memory_space=pl.ANY)
    pooled_grad, proj_grad, loss = pl.pallas_call(
        kernel,
        out_shape=(
            jax.ShapeDtypeStruct((CAP, D), BF16),
            jax.ShapeDtypeStruct((32, F), F32),
            jax.ShapeDtypeStruct((1, 128), F32),
        ),
        in_specs=[hbm, vm, vm, hbm],
        out_specs=(vm, vm, vm),
        scratch_shapes=[
            pltpu.VMEM((4, TOK, 1024), BF16),
            pltpu.VMEM((D, F), BF16),
            pltpu.VMEM((16, CAP, 256), BF16),
            pltpu.VMEM((COLS, 256), BF16),
            pltpu.VMEM((2, 2, COLS, 256), BF16),
            pltpu.VMEM((2, 2, ROWS, 256), BF16),
            pltpu.VMEM((2, 2, COLS, 256), BF16),
            pltpu.VMEM((ROWS, COLS), F32),
            pltpu.VMEM((ROWS, COLS), BF16),
            pltpu.VMEM((ROWS, 128), F32),
            pltpu.VMEM((COLS, 128), F32),
            pltpu.VMEM((16, 1, EXTRA), F32),
            pltpu.VMEM((8, 1, ROWS), F32),
            pltpu.VMEM((8, 1, 128), F32),
            pltpu.VMEM((1, COLS), F32),
            pltpu.VMEM((CAP, F), F32),
            pltpu.VMEM((CAP, F), F32),
        ]
        + reduce_scratch(CAP, BF16)
        + [
            pltpu.VMEM((4, 4, 2, 32, 256), F32),
            pltpu.VMEM((4, 4, 32, 256), BF16),
            pltpu.VMEM((4, 4, 32, 256), BF16),
            pltpu.VMEM((3, 4, 32, 256), BF16),
            pltpu.VMEM((3, 4, 32, 256), BF16),
        ]
        + [
            dma((2, 4)),
            dma((4, 10)), dma((4, 10)), dma((3, 7)), dma((3, 7)), dma((4, 10)), dma((4, 10)),
            dma((4, 4)), dma((4, 4)), dma((4,)), dma((4,)),
            dma((15,)), dma((15,)), dma((15,)), dma((15,)), dma((7,)), dma((7,)), dma((7,)), dma((7,)),
        ],
        compiler_params=pltpu.CompilerParams(
            collective_id=0, has_side_effects=True, vmem_limit_bytes=60 * 1024 * 1024
        ),
        cost_estimate=pl.CostEstimate(flops=6_000_000_000, bytes_accessed=14_000_000, transcendentals=2_000_000),
    )(hidden, slots, positive.reshape(1, CAP), proj)
    onehot = (step_slot[None, :] == lax.broadcasted_iota(jnp.int32, (CAP, TOK), 0)).astype(BF16)
    hidden_grad = lax.dot_general(onehot, pooled_grad, (((0,), (0,)), ((), ())), preferred_element_type=F32)
    return (hidden_grad.astype(BF16), proj_grad, loss[0, 0])


def solution(mesh):
    in_specs = (P(("dp", "rep"), None), P(("dp", "rep")), P(("dp", "rep")), P())
    out_specs = (P(("dp", "rep"), None), P(("dp", "rep"), None), P())
    return jax.shard_map(local, mesh=mesh, in_specs=in_specs, out_specs=out_specs, check_vma=False)
```

```python
import functools
import math

import jax
import jax.numpy as jnp
from jax import lax
from jax.experimental import pallas as pl
from jax.experimental.pallas import tpu as pltpu
from jax.sharding import PartitionSpec as P

MESH = pl.DeviceIdType.MESH
F32 = jnp.float32
BF16 = jnp.bfloat16
CAP = 80
TOK = 384
D = 4096
F = 1024
ROWS = 640
COLS = 1280
EXTRA = COLS + 128
MULT = 1.0 / (0.3 * math.sqrt(F))
LOG2E = 1.4426950408889634
NEG = -1e30
MARK = 256.0


def rcopy(src, dst, send_sem, recv_sem, device):
    return pltpu.make_async_remote_copy(
        src_ref=src, dst_ref=dst, send_sem=send_sem, recv_sem=recv_sem, device_id=device, device_id_type=MESH
    )


class GatherDp:
    def __init__(self, buf, ssem, rsem, z, y, rep):
        self.buf, self.ssem, self.rsem = buf, ssem, rsem
        self.z = [z, (z + 1) % 4, (z + 2) % 4, (z + 3) % 4]
        self.y = [y, (y + 1) % 4, (y + 2) % 4, (y + 3) % 4]
        self.dev = [
            (self.z[1] * 4 + y, rep),
            (self.z[3] * 4 + y, rep),
            (z * 4 + self.y[1], rep),
            (z * 4 + self.y[3], rep),
        ]
        self.copies = {}

    def at(self, dz, dy):
        return pl.ds(pl.multiple_of((self.z[dz % 4] * 4 + self.y[dy % 4]) * CAP, CAP), CAP)

    def send(self, direction, slot, h, d, dz, dy):
        piece = self.buf.at[h, d, self.at(dz, dy)]
        c = rcopy(piece, piece, self.ssem.at[direction, slot], self.rsem.at[direction, slot], self.dev[direction])
        c.start()
        self.copies[direction, slot] = c

    def recv(self, *which):
        for w in which:
            self.copies[w].wait_recv()

    def start(self, h):
        a = slice(None)
        for direction in (0, 1) if h == 0 else (2, 3):
            self.send(direction, 0, h, a, 0, 0)
        for direction in (2, 3) if h == 0 else (0, 1):
            self.send(direction, 8, h, a, 0, 0)

    def first(self, h):
        a = slice(None)
        if h == 0:
            self.recv((0, 0))
            self.send(0, 1, 0, 0, -1, 0)
            self.send(2, 2, 0, a, -1, 0)
            self.send(3, 2, 0, a, -1, 0)
            self.recv((1, 0))
            self.send(1, 1, 0, 1, 1, 0)
            self.send(2, 3, 0, a, 1, 0)
            self.send(3, 3, 0, a, 1, 0)
        else:
            self.recv((2, 0))
            self.send(2, 1, 1, 0, 0, -1)
            self.send(0, 2, 1, a, 0, -1)
            self.send(1, 2, 1, a, 0, -1)
            self.recv((3, 0))
            self.send(3, 1, 1, 1, 0, 1)
            self.send(0, 3, 1, a, 0, 1)
            self.send(1, 3, 1, a, 0, 1)

    def second(self, h):
        if h == 0:
            self.recv((2, 8))
            self.send(2, 9, 0, 0, 0, -1)
            self.recv((3, 8))
            self.send(3, 9, 0, 1, 0, 1)
        else:
            self.recv((0, 8))
            self.send(0, 9, 1, 0, -1, 0)
            self.recv((1, 8))
            self.send(1, 9, 1, 1, 1, 0)

    def far(self, h):
        a = slice(None)
        if h == 0:
            self.recv((0, 1), (1, 1))
            self.send(2, 4, 0, a, 2, 0)
            self.send(3, 4, 0, a, 2, 0)
        else:
            self.recv((2, 1), (3, 1))
            self.send(0, 4, 1, a, 0, 2)
            self.send(1, 4, 1, a, 0, 2)

    def cross(self, h):
        if h == 0:
            self.recv((2, 2))
            self.send(2, 5, 0, 0, -1, -1)
            self.recv((3, 2))
            self.send(3, 5, 0, 1, -1, 1)
            self.recv((2, 3))
            self.send(2, 6, 0, 0, 1, -1)
            self.recv((3, 3))
            self.send(3, 6, 0, 1, 1, 1)
        else:
            self.recv((0, 2))
            self.send(0, 5, 1, 0, -1, -1)
            self.recv((1, 2))
            self.send(1, 5, 1, 1, 1, -1)
            self.recv((0, 3))
            self.send(0, 6, 1, 0, -1, 1)
            self.recv((1, 3))
            self.send(1, 6, 1, 1, 1, 1)

    def last(self, h):
        if h == 0:
            self.recv((2, 4))
            self.send(2, 7, 0, 0, 2, -1)
            self.recv((3, 4))
            self.send(3, 7, 0, 1, 2, 1)
        else:
            self.recv((0, 4))
            self.send(0, 7, 1, 0, -1, 2)
            self.recv((1, 4))
            self.send(1, 7, 1, 1, 1, 2)

    def drain(self):
        for c in self.copies.values():
            c.wait_send()


class GatherRep:
    def __init__(self, buf, ssem, rsem, dp, x, k):
        self.buf, self.ssem, self.rsem, self.k = buf, ssem, rsem, k
        self.x = [x, (x + 1) % 4, (x + 2) % 4, (x + 3) % 4]
        self.dev = [(dp, self.x[1] * 2 + k), (dp, self.x[3] * 2 + k), (dp, x * 2 + 1 - k)]
        self.copies = {}

    def send(self, direction, slot, u, dx):
        at = pl.ds(pl.multiple_of((self.x[dx % 4] * 2 + self.k) * CAP, CAP), CAP)
        piece = self.buf.at[u, :, at]
        c = rcopy(piece, piece, self.ssem.at[direction, slot], self.rsem.at[direction, slot], self.dev[direction])
        c.start()
        self.copies[direction, slot] = c

    def recv(self, *which):
        for w in which:
            self.copies[w].wait_recv()

    def round1(self):
        self.send(0, 0, 0, 0)
        self.send(1, 0, 1, 0)
        self.send(0, 2, 1, 0)
        self.send(1, 2, 0, 0)
        self.send(2, 0, slice(None), 0)

    def round2(self):
        self.recv((0, 0))
        self.send(0, 1, 0, -1)
        self.send(2, 1, 0, -1)
        self.recv((1, 0))
        self.send(1, 1, 1, 1)
        self.send(2, 2, 1, 1)

    def round3(self):
        self.recv((0, 2))
        self.send(2, 3, 1, -1)
        self.recv((1, 2))
        self.send(2, 4, 0, 1)

    def round4(self):
        self.recv((0, 1))
        self.send(2, 5, 0, 2)
        self.recv((1, 1))
        self.send(2, 6, 1, 2)

    def finish(self):
        for slot in range(7):
            self.recv((2, slot))

    def drain(self):
        for c in self.copies.values():
            c.wait_send()


class ReduceRep:
    def __init__(self, full, out, sib, far, far_in, near, near_in, mid, mid_in, ssem, rsem, dp, x, k):
        self.full, self.out, self.sib = full, out, sib
        self.far, self.far_in, self.near, self.near_in, self.mid, self.mid_in = far, far_in, near, near_in, mid, mid_in
        self.ssem, self.rsem, self.k = ssem, rsem, k
        self.x = [x, (x + 1) % 4, (x + 2) % 4, (x + 3) % 4]
        self.right, self.left = (dp, self.x[1] * 2 + k), (dp, self.x[3] * 2 + k)
        self.other = (dp, x * 2 + 1 - k)
        self.copies = {}

    def send(self, kind, q, src, dst, device):
        c = rcopy(src, dst, self.ssem.at[kind, q], self.rsem.at[kind, q], device)
        c.start()
        self.copies[kind, q] = c

    def put(self, q, value):
        parts = value.reshape((4, 2) + (value.shape[0] // 8, 256))
        self.full[q] = parts
        self.out[q] = parts.astype(self.out.dtype)
        self.send(0, q, self.out.at[q, :, 1 - self.k], self.sib.at[q], self.other)

    def part(self, q, dx):
        at = self.x[dx % 4]
        return self.full[q, at, self.k] + self.sib[q, at].astype(F32)

    def step1(self, q):
        self.copies[0, q].wait_recv()
        ahead, behind = (self.right, self.left) if q < 2 else (self.left, self.right)
        self.far[q] = self.part(q, 2).astype(self.far.dtype)
        self.send(1, q, self.far.at[q], self.far_in.at[q], ahead)
        self.near[q] = self.part(q, -1 if q < 2 else 1).astype(self.near.dtype)
        self.send(2, q, self.near.at[q], self.near_in.at[q], behind)

    def step2(self, q):
        self.copies[1, q].wait_recv()
        self.mid[q] = (self.part(q, 1 if q < 2 else -1) + self.far_in[q].astype(F32)).astype(self.mid.dtype)
        self.send(3, q, self.mid.at[q], self.mid_in.at[q], self.right if q < 2 else self.left)

    def result(self, q):
        self.copies[2, q].wait_recv()
        self.copies[3, q].wait_recv()
        return self.part(q, 0) + self.near_in[q].astype(F32) + self.mid_in[q].astype(F32)

    def drain(self):
        for c in self.copies.values():
            c.wait_send()


ORDER = (0, 2, 1, 3)


def kernel(
    hidden_hbm, slot_ref, pos_ref, proj_hbm,
    pgrad_out, proj_out, part_out1, part_out2, part_out3, loss_out,
    hid, proj, pooled, pooled_in, uc, ur, ec, scores, weights, rowsum, colpart, zc, zr, zl, bias_c,
    posterm, unit_s,
    g_full, g_out, g_sib, g_far, g_far_in, g_near, g_near_in, g_mid, g_mid_in,
    p_full, p_out, p_sib,
    load_sem, uc_s, uc_r, ur_s, ur_r, ec_s, ec_r, g_s, g_r, p_s, p_r, a2a_s, a2a_r, zc_s, zc_r, zr_s, zr_r, zl_s, zl_r,
):
    dp, rep = lax.axis_index("dp"), lax.axis_index("rep")
    z, y, x, k = dp // 4, dp % 4, rep // 2, rep % 2
    dp_peers = [((dp + j) % 16, rep) for j in range(1, 16)]
    rep_peers = [(dp, (rep + j) % 8) for j in range(1, 8)]

    loads = []
    for j in range(4):
        loads.append(
            (
                pltpu.make_async_copy(hidden_hbm.at[:, pl.ds(j * 1024, 1024)], hid.at[j], load_sem.at[0, j]),
                pltpu.make_async_copy(proj_hbm.at[pl.ds(j * 1024, 1024)], proj.at[pl.ds(j * 1024, 1024)], load_sem.at[1, j]),
            )
        )
        loads[-1][0].start()
        loads[-1][1].start()

    barrier = pltpu.get_barrier_semaphore()
    near = [((z + 1) % 4 * 4 + y, rep), ((z + 3) % 4 * 4 + y, rep), (z * 4 + (y + 1) % 4, rep), (z * 4 + (y + 3) % 4, rep)]
    near += [(dp, (x + 1) % 4 * 2 + k), (dp, (x + 3) % 4 * 2 + k), (dp, x * 2 + 1 - k)]
    for peer in near:
        pl.semaphore_signal(barrier, inc=1, device_id=peer, device_id_type=MESH)

    member = slot_ref[...].reshape(1, TOK) == lax.broadcasted_iota(jnp.int32, (CAP, TOK), 0)
    onehot = member.astype(F32)
    counts = jnp.sum(onehot, axis=1, keepdims=True)
    onehot = onehot.astype(BF16)
    denom = jnp.maximum(counts, 1.0)
    live = counts > 0.0
    embed = jnp.zeros((CAP, F), F32)
    for j in range(4):
        loads[j][0].wait()
        chunk = (jnp.dot(onehot, hid[j], preferred_element_type=F32) / denom).astype(BF16)
        for i in range(4):
            pooled[j * 4 + i] = chunk[:, i * 256 : (i + 1) * 256]
        loads[j][1].wait()
        embed = embed + jnp.dot(chunk, proj[pl.ds(j * 1024, 1024), :], preferred_element_type=F32)
    rscale = lax.rsqrt(jnp.mean(embed * embed, axis=1, keepdims=True) + 1e-06)
    unit = embed * rscale
    unit_s[...] = unit
    unit_b = unit.astype(BF16)
    lane = lax.broadcasted_iota(jnp.int32, (CAP, F), 1)
    marked = jnp.where(jnp.logical_and(lane == 0, jnp.logical_not(live)), MARK, unit).astype(BF16)
    at_c = pl.ds(pl.multiple_of(dp * CAP, CAP), CAP)
    at_r = pl.ds(pl.multiple_of(rep * CAP, CAP), CAP)
    for q in range(4):
        piece = marked[:, q * 256 : (q + 1) * 256]
        uc[q // 2, q % 2, at_c, :] = piece
        ur[q // 2, q % 2, at_r, :] = piece

    pl.semaphore_wait(barrier, 7)

    gc = GatherDp(uc, uc_s, uc_r, z, y, rep)
    gr = GatherRep(ur, ur_s, ur_r, dp, x, k)
    gc.start(0)
    gc.start(1)
    gr.round1()

    at_pos = pos_ref[...] - (dp * 8 + rep) * CAP
    row80 = lax.broadcasted_iota(jnp.int32, (CAP, CAP), 0)
    col80 = lax.broadcasted_iota(jnp.int32, (CAP, CAP), 1)
    back = jnp.where(jnp.logical_and(at_pos == row80, row80 != col80), 1.0, 0.0).astype(BF16)
    partner = lax.dot_general(back, unit_b, (((0,), (0,)), ((), ())), preferred_element_type=F32)
    posterm[...] = partner + jnp.dot(back, unit_b, preferred_element_type=F32)
    picked = jnp.sum(jnp.sum(partner * unit_b.astype(F32), axis=1, keepdims=True), axis=0, keepdims=True) * MULT

    def pair_sums(blocks, own):
        cols = jnp.concatenate(
            [jnp.concatenate([uc[q // 2, q % 2, gc.at(*b), :] for q in range(4)], axis=1) for b in blocks], axis=0
        )
        bias = jnp.where(cols[:, 0:1].astype(F32) < 128.0, 0.0, NEG)
        s = lax.dot_general(cols, rows, (((1,), (1,)), ((), ())), preferred_element_type=F32) * (MULT * LOG2E)
        s = s + bias + bias_l
        if own:
            lane = lax.broadcasted_iota(jnp.int32, (CAP, ROWS), 1) - rep * CAP
            s = jnp.where(lane == lax.broadcasted_iota(jnp.int32, (CAP, ROWS), 0), NEG, s)
        e = jnp.exp2(s)
        part = e[:, :128]
        for i in range(1, 5):
            part = part + e[:, i * 128 : (i + 1) * 128]
        for i, b in enumerate(blocks):
            colpart[gc.at(*b), :] = part[i * CAP : (i + 1) * CAP]
        return jnp.sum(e, axis=0, keepdims=True)

    gc.first(0)
    gc.first(1)
    gr.round2()
    gc.far(0)
    gc.far(1)
    gr.round3()
    gc.second(0)
    gc.second(1)
    gr.round4()
    gc.cross(0)
    gc.cross(1)
    gr.finish()
    rows = jnp.concatenate([ur[q // 2, q % 2] for q in range(4)], axis=1)
    live_r = ur[0, 0, :, 0:1].astype(F32) < 128.0
    bias_r = jnp.where(live_r, 0.0, NEG)
    pick0 = jnp.where(lax.broadcasted_iota(jnp.int32, (16, 256), 1) == 0, 1.0, 0.0).astype(BF16)
    first = lax.dot_general(pick0, ur[0, 0], (((1,), (1,)), ((), ())), preferred_element_type=F32)
    bias_l = jnp.where(first[0:1] < 128.0, 0.0, NEG)
    nlive_r = jnp.sum(jnp.where(bias_l < -1.0, 0.0, 1.0), axis=1, keepdims=True)
    sum_r = pair_sums([(0, 0)], True)
    gc.last(0)
    gc.last(1)
    sum_r = sum_r + pair_sums([(-1, 0), (1, 0), (0, -1), (0, 1)], False)
    for direction in range(4):
        gc.recv((direction, 9))
    sum_r = sum_r + pair_sums([(-1, -1), (-1, 1), (1, -1), (1, 1), (2, 0), (0, 2)], False)
    for slot in (5, 6):
        for direction in range(4):
            gc.recv((direction, slot))
    sum_r = sum_r + pair_sums([(-1, 2), (1, 2), (2, -1), (2, 1)], False)
    for direction in range(4):
        gc.recv((direction, 7))
    sum_r = sum_r + pair_sums([(2, 2)], False)
    zr[rep] = sum_r
    zc[dp, :, pl.ds(0, COLS)] = jnp.sum(colpart[...].T, axis=0, keepdims=True)
    l128 = lax.broadcasted_iota(jnp.int32, (1, 128), 1)
    zc[dp, :, pl.ds(COLS, 128)] = jnp.where(l128 == 0, nlive_r, jnp.where(l128 == 1, picked, 0.0))

    zcopies = []
    for j in range(15):
        zcopies.append(rcopy(zc.at[dp], zc.at[dp], zc_s.at[j], zc_r.at[j], dp_peers[j]))
        zcopies[-1].start()
    for j in range(7):
        zcopies.append(rcopy(zr.at[rep], zr.at[rep], zr_s.at[j], zr_r.at[j], rep_peers[j]))
        zcopies[-1].start()

    id_r = lax.broadcasted_iota(jnp.int32, (ROWS, 1), 0) - rep * CAP
    id_r = jnp.where(jnp.logical_and(id_r >= 0, id_r < CAP), id_r, -1)

    def score_tile(t, carry):
        at = pl.ds(pl.multiple_of(t * 256, 256), 256)
        cols = jnp.concatenate([uc[q // 2, q % 2, at, :] for q in range(4)], axis=1)
        first = lax.dot_general(pick0, cols[:, :256], (((1,), (1,)), ((), ())), preferred_element_type=F32)
        bias = jnp.where(first[0:1] < 128.0, 0.0, NEG)
        bias_c[:, at] = bias
        id_c = lax.broadcasted_iota(jnp.int32, (1, 256), 1) + t * 256 - dp * CAP
        id_c = jnp.where(jnp.logical_and(id_c >= 0, id_c < CAP), id_c, -2)
        s = lax.dot_general(rows, cols, (((1,), (1,)), ((), ())), preferred_element_type=F32) * (MULT * LOG2E)
        scores[:, at] = jnp.where(id_r == id_c, NEG, s + bias_r + bias)
        return carry

    lax.fori_loop(0, 5, score_tile, 0)
    for c in zcopies:
        c.wait_recv()

    total_c = zc[0]
    for j in range(1, 16):
        total_c = total_c + zc[j]
    total_r = zr[0]
    for j in range(1, 8):
        total_r = total_r + zr[j]
    nlive = total_c[:, COLS : COLS + 1]
    log_c = jnp.where(bias_c[...] < -1.0, 0.0, jnp.log(total_c[:, :COLS]))
    bias_c[...] = log_c * LOG2E
    log_r = jnp.broadcast_to(jnp.log(total_r) * LOG2E, (128, ROWS)).T
    log_r = jnp.where(live_r, log_r, 0.0)
    rowsum[...] = log_r

    def weight_tile(t, carry):
        at = pl.ds(pl.multiple_of(t * 128, 128), 128)
        s = scores[:, at]
        w = jnp.exp2(s - rowsum[...]) + jnp.exp2(s - bias_c[:, at])
        weights[:, at] = w.astype(BF16)
        return carry

    lax.fori_loop(0, 10, weight_tile, 0)

    red = ReduceRep(g_full, g_out, g_sib, g_far, g_far_in, g_near, g_near_in, g_mid, g_mid_in, g_s, g_r, dp, x, k)
    for q in ORDER:
        red.put(q, jnp.dot(weights[...], uc[q // 2, q % 2], preferred_element_type=F32))
    for q in ORDER:
        red.step1(q)
    a2a = []
    for j in range(15):
        peer = dp_peers[j]
        c = rcopy(pooled.at[peer[0]], pooled_in.at[at_c], a2a_s.at[j], a2a_r.at[j], peer)
        c.start()
        a2a.append(c)
    pooled_in[at_c, :] = pooled[dp]

    for q in ORDER:
        red.step2(q)
    loss_c = jnp.sum(log_c, axis=1, keepdims=True) - total_c[:, COLS + 1 : COLS + 2]
    zl[rep] = jnp.broadcast_to(loss_c, (1, 128))
    lcopies = []
    for j in range(7):
        lcopies.append(rcopy(zl.at[rep], zl.at[rep], zl_s.at[j], zl_r.at[j], rep_peers[j]))
        lcopies[-1].start()
    got = jnp.concatenate([red.result(q) for q in range(4)], axis=1)
    unit = unit_s[...]
    ugrad = (got - posterm[...]) * (MULT / nlive)
    inner = jnp.mean(unit * ugrad, axis=1, keepdims=True)
    egrad = (rscale * (ugrad - unit * inner)).astype(BF16)
    for q in range(4):
        ec[q // 2, q % 2, at_c, :] = egrad[:, q * 256 : (q + 1) * 256]

    ge = GatherDp(ec, ec_s, ec_r, z, y, rep)

    def pgrad(j):
        at = pl.ds(j * 512, 512)
        part = lax.dot_general(egrad, proj[at, :], (((1,), (1,)), ((), ())), preferred_element_type=F32)
        pgrad_out[:, at] = (part / denom).astype(BF16)

    def proj_part(blocks, begin=False):
        left = jnp.concatenate([pooled_in[ge.at(*b), :] for b in blocks], axis=0).astype(F32).T.astype(BF16)
        for q in range(4):
            right = jnp.concatenate([ec[q // 2, q % 2, ge.at(*b), :] for b in blocks], axis=0)
            part = jnp.dot(left, right, preferred_element_type=F32).reshape(4, 2, 32, 256)
            p_full[q] = part if begin else p_full[q] + part

    ge.start(0)
    ge.start(1)
    for c in a2a:
        c.wait_recv()
    proj_part([(0, 0)], True)
    ge.first(0)
    ge.first(1)
    pgrad(0)
    ge.far(0)
    ge.far(1)
    ge.second(0)
    ge.second(1)
    pgrad(1)
    pgrad(2)
    ge.cross(0)
    ge.cross(1)
    pgrad(3)
    ge.last(0)
    ge.last(1)
    for j in range(4, 8):
        pgrad(j)
    proj_part([(-1, 0), (1, 0), (0, -1), (0, 1)])
    for direction in range(4):
        ge.recv((direction, 9))
    proj_part([(-1, -1), (-1, 1), (1, -1), (1, 1), (2, 0), (0, 2)])
    for slot in (5, 6):
        for direction in range(4):
            ge.recv((direction, slot))
    proj_part([(-1, 2), (1, 2), (2, -1), (2, 1)])
    for direction in range(4):
        ge.recv((direction, 7))
    proj_part([(2, 2)])

    p_out[...] = p_full[:, :, 1 - k].astype(BF16)
    pcopy = rcopy(p_out, p_sib, p_s.at[3], p_r.at[3], (dp, x * 2 + 1 - k))
    pcopy.start()
    pcopy.wait_recv()
    part_outs = (part_out1, part_out2, part_out3)
    for j in range(1, 4):
        to = (x + j) % 4
        part = (p_full[:, to, k] + p_sib[:, to].astype(F32)).astype(BF16)
        for q in range(4):
            part_outs[j - 1][:, q * 256 : (q + 1) * 256] = part[q]
    total = p_full[:, x, k] + p_sib[:, x].astype(F32)
    for q in range(4):
        proj_out[:, q * 256 : (q + 1) * 256] = total[q]

    for c in lcopies:
        c.wait_recv()
    loss = zl[0]
    for j in range(1, 8):
        loss = loss + zl[j]
    loss_out[...] = loss / nlive

    for group in (gc, gr, red, ge):
        group.drain()
    for c in a2a + zcopies + lcopies + [pcopy]:
        c.wait_send()


def reduce_scratch(n, kind):
    return [pltpu.VMEM((4, 4, 2, n, 256), F32), pltpu.VMEM((4, 4, 2, n, 256), kind), pltpu.VMEM((4, 4, n, 256), kind)] + [
        pltpu.VMEM((4, n, 256), kind) for _ in range(6)
    ]


def local(hidden, step_slot, positive, proj):
    dma = pltpu.SemaphoreType.DMA
    vm = pl.BlockSpec(memory_space=pltpu.VMEM)
    hbm = pl.BlockSpec(memory_space=pl.ANY)
    pooled_grad, proj_grad, part1, part2, part3, loss = pl.pallas_call(
        kernel,
        out_shape=(
            jax.ShapeDtypeStruct((CAP, D), BF16),
            jax.ShapeDtypeStruct((32, F), F32),
            jax.ShapeDtypeStruct((32, F), BF16),
            jax.ShapeDtypeStruct((32, F), BF16),
            jax.ShapeDtypeStruct((32, F), BF16),
            jax.ShapeDtypeStruct((1, 128), F32),
        ),
        in_specs=[hbm, vm, vm, hbm],
        out_specs=(vm,) * 6,
        scratch_shapes=[
            pltpu.VMEM((4, TOK, 1024), BF16),
            pltpu.VMEM((D, F), BF16),
            pltpu.VMEM((16, CAP, 256), BF16),
            pltpu.VMEM((COLS, 256), BF16),
            pltpu.VMEM((2, 2, COLS, 256), BF16),
            pltpu.VMEM((2, 2, ROWS, 256), BF16),
            pltpu.VMEM((2, 2, COLS, 256), BF16),
            pltpu.VMEM((ROWS, COLS), F32),
            pltpu.VMEM((ROWS, COLS), BF16),
            pltpu.VMEM((ROWS, 128), F32),
            pltpu.VMEM((COLS, 128), F32),
            pltpu.VMEM((16, 1, EXTRA), F32),
            pltpu.VMEM((8, 1, ROWS), F32),
            pltpu.VMEM((8, 1, 128), F32),
            pltpu.VMEM((1, COLS), F32),
            pltpu.VMEM((CAP, F), F32),
            pltpu.VMEM((CAP, F), F32),
        ]
        + reduce_scratch(CAP, BF16)
        + [
            pltpu.VMEM((4, 4, 2, 32, 256), F32),
            pltpu.VMEM((4, 4, 32, 256), BF16),
            pltpu.VMEM((4, 4, 32, 256), BF16),
        ]
        + [
            dma((2, 4)),
            dma((4, 10)), dma((4, 10)), dma((3, 7)), dma((3, 7)), dma((4, 10)), dma((4, 10)),
            dma((4, 4)), dma((4, 4)), dma((4,)), dma((4,)),
            dma((15,)), dma((15,)), dma((15,)), dma((15,)), dma((7,)), dma((7,)), dma((7,)), dma((7,)),
        ],
        compiler_params=pltpu.CompilerParams(
            collective_id=0, has_side_effects=True, vmem_limit_bytes=60 * 1024 * 1024
        ),
        cost_estimate=pl.CostEstimate(flops=6_000_000_000, bytes_accessed=14_000_000, transcendentals=2_000_000),
    )(hidden, step_slot, positive.reshape(1, CAP), proj)
    for j, part in ((1, part1), (3, part3), (2, part2)):
        ring = [(d, (d // 2 + j) % 4 * 2 + d % 2) for d in range(8)]
        proj_grad = proj_grad + lax.ppermute(part, "rep", ring).astype(F32)
    onehot = (step_slot[None, :] == lax.broadcasted_iota(jnp.int32, (CAP, TOK), 0)).astype(BF16)
    hidden_grad = lax.dot_general(onehot, pooled_grad, (((0,), (0,)), ((), ())), preferred_element_type=F32)
    return (hidden_grad.astype(BF16), proj_grad, loss[0, 0])


def solution(mesh):
    in_specs = (P(("dp", "rep"), None), P(("dp", "rep")), P(("dp", "rep")), P())
    out_specs = (P(("dp", "rep"), None), P(("dp", "rep"), None), P())
    return jax.shard_map(local, mesh=mesh, in_specs=in_specs, out_specs=out_specs, check_vma=False)
```

```python
import functools
import math

import jax
import jax.numpy as jnp
from jax import lax
from jax.experimental import pallas as pl
from jax.experimental.pallas import tpu as pltpu
from jax.sharding import PartitionSpec as P

MESH = pl.DeviceIdType.MESH
F32 = jnp.float32
BF16 = jnp.bfloat16
CAP = 80
TOK = 384
D = 4096
F = 1024
ROWS = 640
COLS = 1280
EXTRA = COLS + 128
MULT = 1.0 / (0.3 * math.sqrt(F))
LOG2E = 1.4426950408889634
NEG = -1e30
MARK = 256.0


def rcopy(src, dst, send_sem, recv_sem, device):
    return pltpu.make_async_remote_copy(
        src_ref=src, dst_ref=dst, send_sem=send_sem, recv_sem=recv_sem, device_id=device, device_id_type=MESH
    )


FLIGHT = 8
GRP = 2


class GatherDp:
    def __init__(self, buf, ssem, rsem, z, y, rep):
        self.buf, self.ssem, self.rsem = buf, ssem, rsem
        self.z = [z, (z + 1) % 4, (z + 2) % 4, (z + 3) % 4]
        self.y = [y, (y + 1) % 4, (y + 2) % 4, (y + 3) % 4]
        self.dev = [
            (self.z[1] * 4 + y, rep),
            (self.z[3] * 4 + y, rep),
            (z * 4 + self.y[1], rep),
            (z * 4 + self.y[3], rep),
        ]
        self.copies = {}

    def at(self, dz, dy):
        return pl.ds(pl.multiple_of((self.z[dz % 4] * 4 + self.y[dy % 4]) * CAP, CAP), CAP)

    def send(self, direction, slot, h, d, dz, dy):
        piece = self.buf.at[h, d, self.at(dz, dy)]
        c = rcopy(piece, piece, self.ssem.at[direction, slot], self.rsem.at[direction, slot], self.dev[direction])
        c.start()
        self.copies[direction, slot] = c

    def recv(self, *which):
        for w in which:
            self.copies[w].wait_recv()

    def start(self, h):
        a = slice(None)
        for direction in (0, 1) if h == 0 else (2, 3):
            self.send(direction, 0, h, a, 0, 0)
        for direction in (2, 3) if h == 0 else (0, 1):
            self.send(direction, 8, h, a, 0, 0)

    def first(self, h):
        a = slice(None)
        if h == 0:
            self.recv((0, 0))
            self.send(0, 1, 0, 0, -1, 0)
            self.send(2, 2, 0, a, -1, 0)
            self.send(3, 2, 0, a, -1, 0)
            self.recv((1, 0))
            self.send(1, 1, 0, 1, 1, 0)
            self.send(2, 3, 0, a, 1, 0)
            self.send(3, 3, 0, a, 1, 0)
        else:
            self.recv((2, 0))
            self.send(2, 1, 1, 0, 0, -1)
            self.send(0, 2, 1, a, 0, -1)
            self.send(1, 2, 1, a, 0, -1)
            self.recv((3, 0))
            self.send(3, 1, 1, 1, 0, 1)
            self.send(0, 3, 1, a, 0, 1)
            self.send(1, 3, 1, a, 0, 1)

    def second(self, h):
        if h == 0:
            self.recv((2, 8))
            self.send(2, 9, 0, 0, 0, -1)
            self.recv((3, 8))
            self.send(3, 9, 0, 1, 0, 1)
        else:
            self.recv((0, 8))
            self.send(0, 9, 1, 0, -1, 0)
            self.recv((1, 8))
            self.send(1, 9, 1, 1, 1, 0)

    def far(self, h):
        a = slice(None)
        if h == 0:
            self.recv((0, 1), (1, 1))
            self.send(2, 4, 0, a, 2, 0)
            self.send(3, 4, 0, a, 2, 0)
        else:
            self.recv((2, 1), (3, 1))
            self.send(0, 4, 1, a, 0, 2)
            self.send(1, 4, 1, a, 0, 2)

    def cross(self, h):
        if h == 0:
            self.recv((2, 2))
            self.send(2, 5, 0, 0, -1, -1)
            self.recv((3, 2))
            self.send(3, 5, 0, 1, -1, 1)
            self.recv((2, 3))
            self.send(2, 6, 0, 0, 1, -1)
            self.recv((3, 3))
            self.send(3, 6, 0, 1, 1, 1)
        else:
            self.recv((0, 2))
            self.send(0, 5, 1, 0, -1, -1)
            self.recv((1, 2))
            self.send(1, 5, 1, 1, 1, -1)
            self.recv((0, 3))
            self.send(0, 6, 1, 0, -1, 1)
            self.recv((1, 3))
            self.send(1, 6, 1, 1, 1, 1)

    def last(self, h):
        if h == 0:
            self.recv((2, 4))
            self.send(2, 7, 0, 0, 2, -1)
            self.recv((3, 4))
            self.send(3, 7, 0, 1, 2, 1)
        else:
            self.recv((0, 4))
            self.send(0, 7, 1, 0, -1, 2)
            self.recv((1, 4))
            self.send(1, 7, 1, 1, 1, 2)

    def drain(self):
        for c in self.copies.values():
            c.wait_send()


class GatherRep:
    def __init__(self, buf, ssem, rsem, dp, x, k):
        self.buf, self.ssem, self.rsem, self.k = buf, ssem, rsem, k
        self.x = [x, (x + 1) % 4, (x + 2) % 4, (x + 3) % 4]
        self.dev = [(dp, self.x[1] * 2 + k), (dp, self.x[3] * 2 + k), (dp, x * 2 + 1 - k)]
        self.copies = {}

    def send(self, direction, slot, u, dx):
        at = pl.ds(pl.multiple_of((self.x[dx % 4] * 2 + self.k) * CAP, CAP), CAP)
        piece = self.buf.at[u, :, at]
        c = rcopy(piece, piece, self.ssem.at[direction, slot], self.rsem.at[direction, slot], self.dev[direction])
        c.start()
        self.copies[direction, slot] = c

    def recv(self, *which):
        for w in which:
            self.copies[w].wait_recv()

    def round1(self):
        self.send(0, 0, 0, 0)
        self.send(1, 0, 1, 0)
        self.send(0, 2, 1, 0)
        self.send(1, 2, 0, 0)
        self.send(2, 0, slice(None), 0)

    def round2(self):
        self.recv((0, 0))
        self.send(0, 1, 0, -1)
        self.send(2, 1, 0, -1)
        self.recv((1, 0))
        self.send(1, 1, 1, 1)
        self.send(2, 2, 1, 1)

    def round3(self):
        self.recv((0, 2))
        self.send(2, 3, 1, -1)
        self.recv((1, 2))
        self.send(2, 4, 0, 1)

    def round4(self):
        self.recv((0, 1))
        self.send(2, 5, 0, 2)
        self.recv((1, 1))
        self.send(2, 6, 1, 2)

    def finish(self):
        for slot in range(7):
            self.recv((2, slot))

    def drain(self):
        for c in self.copies.values():
            c.wait_send()


class ReduceRep:
    def __init__(self, full, out, sib, far, far_in, near, near_in, mid, mid_in, ssem, rsem, dp, x, k):
        self.full, self.out, self.sib = full, out, sib
        self.far, self.far_in, self.near, self.near_in, self.mid, self.mid_in = far, far_in, near, near_in, mid, mid_in
        self.ssem, self.rsem, self.k = ssem, rsem, k
        self.x = [x, (x + 1) % 4, (x + 2) % 4, (x + 3) % 4]
        self.right, self.left = (dp, self.x[1] * 2 + k), (dp, self.x[3] * 2 + k)
        self.other = (dp, x * 2 + 1 - k)
        self.copies = {}

    def send(self, kind, q, src, dst, device):
        c = rcopy(src, dst, self.ssem.at[kind, q], self.rsem.at[kind, q], device)
        c.start()
        self.copies[kind, q] = c

    def put(self, q, value):
        parts = value.reshape((4, 2) + (value.shape[0] // 8, 256))
        self.full[q] = parts
        self.out[q] = parts.astype(self.out.dtype)
        self.send(0, q, self.out.at[q, :, 1 - self.k], self.sib.at[q], self.other)

    def part(self, q, dx):
        at = self.x[dx % 4]
        return self.full[q, at, self.k] + self.sib[q, at].astype(F32)

    def step1(self, q):
        self.copies[0, q].wait_recv()
        ahead, behind = (self.right, self.left) if q < 2 else (self.left, self.right)
        self.far[q] = self.part(q, 2).astype(self.far.dtype)
        self.send(1, q, self.far.at[q], self.far_in.at[q], ahead)
        self.near[q] = self.part(q, -1 if q < 2 else 1).astype(self.near.dtype)
        self.send(2, q, self.near.at[q], self.near_in.at[q], behind)

    def step2(self, q):
        self.copies[1, q].wait_recv()
        self.mid[q] = (self.part(q, 1 if q < 2 else -1) + self.far_in[q].astype(F32)).astype(self.mid.dtype)
        self.send(3, q, self.mid.at[q], self.mid_in.at[q], self.right if q < 2 else self.left)

    def result(self, q):
        self.copies[2, q].wait_recv()
        self.copies[3, q].wait_recv()
        return self.part(q, 0) + self.near_in[q].astype(F32) + self.mid_in[q].astype(F32)

    def drain(self):
        for c in self.copies.values():
            c.wait_send()


ORDER = (0, 2, 1, 3)


def kernel(
    hidden_hbm, slot_ref, pos_ref, proj_hbm,
    pgrad_out, proj_out, part_out1, part_out2, part_out3, loss_out,
    hid, proj, pooled, pooled_in, uc, ur, ec, scores, weights, rowsum, colpart, zc, zr, zl, bias_c,
    posterm, unit_s,
    g_full, g_out, g_sib, g_far, g_far_in, g_near, g_near_in, g_mid, g_mid_in,
    p_full, p_out, p_sib,
    load_sem, uc_s, uc_r, ur_s, ur_r, ec_s, ec_r, g_s, g_r, p_s, p_r, a2a_s, a2a_r, zc_s, zc_r, zr_s, zr_r, zl_s, zl_r,
):
    dp, rep = lax.axis_index("dp"), lax.axis_index("rep")
    z, y, x, k = dp // 4, dp % 4, rep // 2, rep % 2
    dp_peers = [((dp + j) % 16, rep) for j in range(1, 16)]
    rep_peers = [(dp, (rep + j) % 8) for j in range(1, 8)]

    hloads = [
        pltpu.make_async_copy(hidden_hbm.at[:, pl.ds(j * 1024, 1024)], hid.at[j], load_sem.at[j]) for j in range(4)
    ]
    ploads = [
        pltpu.make_async_copy(proj_hbm.at[pl.ds(j * 512, 512)], proj.at[pl.ds(j * 512, 512)], load_sem.at[4 + j])
        for j in range(8)
    ]
    for c in hloads + ploads[:FLIGHT]:
        c.start()

    barrier = pltpu.get_barrier_semaphore()
    near = [((z + 1) % 4 * 4 + y, rep), ((z + 3) % 4 * 4 + y, rep), (z * 4 + (y + 1) % 4, rep), (z * 4 + (y + 3) % 4, rep)]
    near += [(dp, (x + 1) % 4 * 2 + k), (dp, (x + 3) % 4 * 2 + k), (dp, x * 2 + 1 - k)]
    for peer in near:
        pl.semaphore_signal(barrier, inc=1, device_id=peer, device_id_type=MESH)

    member = slot_ref[...].reshape(1, TOK) == lax.broadcasted_iota(jnp.int32, (CAP, TOK), 0)
    onehot = member.astype(F32)
    counts = jnp.sum(onehot, axis=1, keepdims=True)
    onehot = onehot.astype(BF16)
    denom = jnp.maximum(counts, 1.0)
    live = counts > 0.0
    embed = jnp.zeros((CAP, F), F32)
    chunks = []
    for j in range(4):
        hloads[j].wait()
        chunk = (jnp.dot(onehot, hid[j], preferred_element_type=F32) / denom).astype(BF16)
        for i in range(4):
            pooled[j * 4 + i] = chunk[:, i * 256 : (i + 1) * 256]
        chunks += [chunk[:, :512], chunk[:, 512:]]
    for j in range(8):
        ploads[j].wait()
        if j + FLIGHT < 8:
            ploads[j + FLIGHT].start()
        embed = embed + jnp.dot(chunks[j], proj[pl.ds(j * 512, 512), :], preferred_element_type=F32)
    rscale = lax.rsqrt(jnp.mean(embed * embed, axis=1, keepdims=True) + 1e-06)
    unit = embed * rscale
    unit_s[...] = unit
    unit_b = unit.astype(BF16)
    lane = lax.broadcasted_iota(jnp.int32, (CAP, F), 1)
    marked = jnp.where(jnp.logical_and(lane == 0, jnp.logical_not(live)), MARK, unit).astype(BF16)
    at_c = pl.ds(pl.multiple_of(dp * CAP, CAP), CAP)
    at_r = pl.ds(pl.multiple_of(rep * CAP, CAP), CAP)
    for q in range(4):
        piece = marked[:, q * 256 : (q + 1) * 256]
        uc[q // 2, q % 2, at_c, :] = piece
        ur[q // 2, q % 2, at_r, :] = piece

    pl.semaphore_wait(barrier, 7)

    gc = GatherDp(uc, uc_s, uc_r, z, y, rep)
    gr = GatherRep(ur, ur_s, ur_r, dp, x, k)
    gc.start(0)
    gc.start(1)
    gr.round1()

    at_pos = pos_ref[...] - (dp * 8 + rep) * CAP
    row80 = lax.broadcasted_iota(jnp.int32, (CAP, CAP), 0)
    col80 = lax.broadcasted_iota(jnp.int32, (CAP, CAP), 1)
    back = jnp.where(jnp.logical_and(at_pos == row80, row80 != col80), 1.0, 0.0).astype(BF16)
    partner = lax.dot_general(back, unit_b, (((0,), (0,)), ((), ())), preferred_element_type=F32)
    posterm[...] = partner + jnp.dot(back, unit_b, preferred_element_type=F32)
    picked = jnp.sum(jnp.sum(partner * unit_b.astype(F32), axis=1, keepdims=True), axis=0, keepdims=True) * MULT

    def pair_sums(blocks, own):
        cols = jnp.concatenate(
            [jnp.concatenate([uc[q // 2, q % 2, gc.at(*b), :] for q in range(4)], axis=1) for b in blocks], axis=0
        )
        bias = jnp.where(cols[:, 0:1].astype(F32) < 128.0, 0.0, NEG)
        s = lax.dot_general(cols, rows, (((1,), (1,)), ((), ())), preferred_element_type=F32) * (MULT * LOG2E)
        s = s + bias + bias_l
        if own:
            lane = lax.broadcasted_iota(jnp.int32, (CAP, ROWS), 1) - rep * CAP
            s = jnp.where(lane == lax.broadcasted_iota(jnp.int32, (CAP, ROWS), 0), NEG, s)
        e = jnp.exp2(s)
        part = e[:, :128]
        for i in range(1, 5):
            part = part + e[:, i * 128 : (i + 1) * 128]
        for i, b in enumerate(blocks):
            colpart[gc.at(*b), :] = part[i * CAP : (i + 1) * CAP]
        return jnp.sum(e, axis=0, keepdims=True)

    gc.first(0)
    gc.first(1)
    gr.round2()
    gc.far(0)
    gc.far(1)
    gr.round3()
    gc.second(0)
    gc.second(1)
    gr.round4()
    gc.cross(0)
    gc.cross(1)
    gr.finish()
    rows = jnp.concatenate([ur[q // 2, q % 2] for q in range(4)], axis=1)
    live_r = ur[0, 0, :, 0:1].astype(F32) < 128.0
    bias_r = jnp.where(live_r, 0.0, NEG)
    pick0 = jnp.where(lax.broadcasted_iota(jnp.int32, (16, 256), 1) == 0, 1.0, 0.0).astype(BF16)
    first = lax.dot_general(pick0, ur[0, 0], (((1,), (1,)), ((), ())), preferred_element_type=F32)
    bias_l = jnp.where(first[0:1] < 128.0, 0.0, NEG)
    nlive_r = jnp.sum(jnp.where(bias_l < -1.0, 0.0, 1.0), axis=1, keepdims=True)
    sum_r = pair_sums([(0, 0)], True)
    gc.last(0)
    gc.last(1)
    sum_r = sum_r + pair_sums([(-1, 0), (1, 0), (0, -1), (0, 1)], False)
    for direction in range(4):
        gc.recv((direction, 9))
    sum_r = sum_r + pair_sums([(-1, -1), (-1, 1), (1, -1), (1, 1), (2, 0), (0, 2)], False)
    for slot in (5, 6):
        for direction in range(4):
            gc.recv((direction, slot))
    sum_r = sum_r + pair_sums([(-1, 2), (1, 2), (2, -1), (2, 1)], False)
    for direction in range(4):
        gc.recv((direction, 7))
    sum_r = sum_r + pair_sums([(2, 2)], False)
    zr[rep] = sum_r
    zc[dp, :, pl.ds(0, COLS)] = jnp.sum(colpart[...].T, axis=0, keepdims=True)
    l128 = lax.broadcasted_iota(jnp.int32, (1, 128), 1)
    zc[dp, :, pl.ds(COLS, 128)] = jnp.where(l128 == 0, nlive_r, jnp.where(l128 == 1, picked, 0.0))

    zcopies = []
    for j in range(15):
        zcopies.append(rcopy(zc.at[dp], zc.at[dp], zc_s.at[j], zc_r.at[j], dp_peers[j]))
        zcopies[-1].start()
    for j in range(7):
        zcopies.append(rcopy(zr.at[rep], zr.at[rep], zr_s.at[j], zr_r.at[j], rep_peers[j]))
        zcopies[-1].start()

    id_r = lax.broadcasted_iota(jnp.int32, (ROWS, 1), 0) - rep * CAP
    id_r = jnp.where(jnp.logical_and(id_r >= 0, id_r < CAP), id_r, -1)

    def score_tile(t, carry):
        at = pl.ds(pl.multiple_of(t * 256, 256), 256)
        cols = jnp.concatenate([uc[q // 2, q % 2, at, :] for q in range(4)], axis=1)
        first = lax.dot_general(pick0, cols[:, :256], (((1,), (1,)), ((), ())), preferred_element_type=F32)
        bias = jnp.where(first[0:1] < 128.0, 0.0, NEG)
        bias_c[:, at] = bias
        id_c = lax.broadcasted_iota(jnp.int32, (1, 256), 1) + t * 256 - dp * CAP
        id_c = jnp.where(jnp.logical_and(id_c >= 0, id_c < CAP), id_c, -2)
        s = lax.dot_general(rows, cols, (((1,), (1,)), ((), ())), preferred_element_type=F32) * (MULT * LOG2E)
        scores[:, at] = jnp.where(id_r == id_c, NEG, s + bias_r + bias)
        return carry

    lax.fori_loop(0, 5, score_tile, 0)
    for c in zcopies:
        c.wait_recv()

    total_c = zc[0]
    for j in range(1, 16):
        total_c = total_c + zc[j]
    total_r = zr[0]
    for j in range(1, 8):
        total_r = total_r + zr[j]
    nlive = total_c[:, COLS : COLS + 1]
    log_c = jnp.where(bias_c[...] < -1.0, 0.0, jnp.log(total_c[:, :COLS]))
    bias_c[...] = log_c * LOG2E
    log_r = jnp.broadcast_to(jnp.log(total_r) * LOG2E, (128, ROWS)).T
    log_r = jnp.where(live_r, log_r, 0.0)
    rowsum[...] = log_r

    def weight_tile(t, carry):
        at = pl.ds(pl.multiple_of(t * 128, 128), 128)
        s = scores[:, at]
        w = jnp.exp2(s - rowsum[...]) + jnp.exp2(s - bias_c[:, at])
        weights[:, at] = w.astype(BF16)
        return carry

    lax.fori_loop(0, 10, weight_tile, 0)

    red = ReduceRep(g_full, g_out, g_sib, g_far, g_far_in, g_near, g_near_in, g_mid, g_mid_in, g_s, g_r, dp, x, k)
    for first_q in range(0, 4, GRP):
        right = jnp.concatenate([uc[q // 2, q % 2] for q in range(first_q, first_q + GRP)], axis=1)
        both = jnp.dot(weights[...], right, preferred_element_type=F32)
        for q in range(GRP):
            red.put(first_q + q, both[:, q * 256 : (q + 1) * 256])
    for q in ORDER:
        red.step1(q)
    a2a = []
    for j in range(15):
        peer = dp_peers[j]
        c = rcopy(pooled.at[peer[0]], pooled_in.at[at_c], a2a_s.at[j], a2a_r.at[j], peer)
        c.start()
        a2a.append(c)
    pooled_in[at_c, :] = pooled[dp]

    for q in ORDER:
        red.step2(q)
    loss_c = jnp.sum(log_c, axis=1, keepdims=True) - total_c[:, COLS + 1 : COLS + 2]
    zl[rep] = jnp.broadcast_to(loss_c, (1, 128))
    lcopies = []
    for j in range(7):
        lcopies.append(rcopy(zl.at[rep], zl.at[rep], zl_s.at[j], zl_r.at[j], rep_peers[j]))
        lcopies[-1].start()
    got = jnp.concatenate([red.result(q) for q in range(4)], axis=1)
    unit = unit_s[...]
    ugrad = (got - posterm[...]) * (MULT / nlive)
    inner = jnp.mean(unit * ugrad, axis=1, keepdims=True)
    egrad = (rscale * (ugrad - unit * inner)).astype(BF16)
    for q in range(4):
        ec[q // 2, q % 2, at_c, :] = egrad[:, q * 256 : (q + 1) * 256]

    ge = GatherDp(ec, ec_s, ec_r, z, y, rep)

    def pgrad(j):
        at = pl.ds(j * 512, 512)
        part = lax.dot_general(egrad, proj[at, :], (((1,), (1,)), ((), ())), preferred_element_type=F32)
        pgrad_out[:, at] = (part / denom).astype(BF16)

    def proj_part(blocks, begin=False):
        left = jnp.concatenate([pooled_in[ge.at(*b), :] for b in blocks], axis=0).astype(F32).T.astype(BF16)
        for q in range(4):
            right = jnp.concatenate([ec[q // 2, q % 2, ge.at(*b), :] for b in blocks], axis=0)
            part = jnp.dot(left, right, preferred_element_type=F32).reshape(4, 2, 32, 256)
            p_full[q] = part if begin else p_full[q] + part

    ge.start(0)
    ge.start(1)
    for c in a2a:
        c.wait_recv()
    proj_part([(0, 0)], True)
    ge.first(0)
    ge.first(1)
    pgrad(0)
    ge.far(0)
    ge.far(1)
    ge.second(0)
    ge.second(1)
    pgrad(1)
    pgrad(2)
    ge.cross(0)
    ge.cross(1)
    pgrad(3)
    ge.last(0)
    ge.last(1)
    for j in range(4, 8):
        pgrad(j)
    proj_part([(-1, 0), (1, 0), (0, -1), (0, 1)])
    for direction in range(4):
        ge.recv((direction, 9))
    proj_part([(-1, -1), (-1, 1), (1, -1), (1, 1), (2, 0), (0, 2)])
    for slot in (5, 6):
        for direction in range(4):
            ge.recv((direction, slot))
    proj_part([(-1, 2), (1, 2), (2, -1), (2, 1)])
    for direction in range(4):
        ge.recv((direction, 7))
    proj_part([(2, 2)])

    p_out[...] = p_full[:, :, 1 - k].astype(BF16)
    pcopy = rcopy(p_out, p_sib, p_s.at[3], p_r.at[3], (dp, x * 2 + 1 - k))
    pcopy.start()
    pcopy.wait_recv()
    part_outs = (part_out1, part_out2, part_out3)
    for j in range(1, 4):
        to = (x + j) % 4
        part = (p_full[:, to, k] + p_sib[:, to].astype(F32)).astype(BF16)
        for q in range(4):
            part_outs[j - 1][:, q * 256 : (q + 1) * 256] = part[q]
    total = p_full[:, x, k] + p_sib[:, x].astype(F32)
    for q in range(4):
        proj_out[:, q * 256 : (q + 1) * 256] = total[q]

    for c in lcopies:
        c.wait_recv()
    loss = zl[0]
    for j in range(1, 8):
        loss = loss + zl[j]
    loss_out[...] = loss / nlive

    for group in (gc, gr, red, ge):
        group.drain()
    for c in a2a + zcopies + lcopies + [pcopy]:
        c.wait_send()


def reduce_scratch(n, kind):
    return [pltpu.VMEM((4, 4, 2, n, 256), F32), pltpu.VMEM((4, 4, 2, n, 256), kind), pltpu.VMEM((4, 4, n, 256), kind)] + [
        pltpu.VMEM((4, n, 256), kind) for _ in range(6)
    ]


def local(hidden, step_slot, positive, proj):
    dma = pltpu.SemaphoreType.DMA
    vm = pl.BlockSpec(memory_space=pltpu.VMEM)
    hbm = pl.BlockSpec(memory_space=pl.ANY)
    pooled_grad, proj_grad, part1, part2, part3, loss = pl.pallas_call(
        kernel,
        out_shape=(
            jax.ShapeDtypeStruct((CAP, D), BF16),
            jax.ShapeDtypeStruct((32, F), F32),
            jax.ShapeDtypeStruct((32, F), BF16),
            jax.ShapeDtypeStruct((32, F), BF16),
            jax.ShapeDtypeStruct((32, F), BF16),
            jax.ShapeDtypeStruct((1, 128), F32),
        ),
        in_specs=[hbm, vm, vm, hbm],
        out_specs=(vm,) * 6,
        scratch_shapes=[
            pltpu.VMEM((4, TOK, 1024), BF16),
            pltpu.VMEM((D, F), BF16),
            pltpu.VMEM((16, CAP, 256), BF16),
            pltpu.VMEM((COLS, 256), BF16),
            pltpu.VMEM((2, 2, COLS, 256), BF16),
            pltpu.VMEM((2, 2, ROWS, 256), BF16),
            pltpu.VMEM((2, 2, COLS, 256), BF16),
            pltpu.VMEM((ROWS, COLS), F32),
            pltpu.VMEM((ROWS, COLS), BF16),
            pltpu.VMEM((ROWS, 128), F32),
            pltpu.VMEM((COLS, 128), F32),
            pltpu.VMEM((16, 1, EXTRA), F32),
            pltpu.VMEM((8, 1, ROWS), F32),
            pltpu.VMEM((8, 1, 128), F32),
            pltpu.VMEM((1, COLS), F32),
            pltpu.VMEM((CAP, F), F32),
            pltpu.VMEM((CAP, F), F32),
        ]
        + reduce_scratch(CAP, BF16)
        + [
            pltpu.VMEM((4, 4, 2, 32, 256), F32),
            pltpu.VMEM((4, 4, 32, 256), BF16),
            pltpu.VMEM((4, 4, 32, 256), BF16),
        ]
        + [
            dma((12,)),
            dma((4, 10)), dma((4, 10)), dma((3, 7)), dma((3, 7)), dma((4, 10)), dma((4, 10)),
            dma((4, 4)), dma((4, 4)), dma((4,)), dma((4,)),
            dma((15,)), dma((15,)), dma((15,)), dma((15,)), dma((7,)), dma((7,)), dma((7,)), dma((7,)),
        ],
        compiler_params=pltpu.CompilerParams(
            collective_id=0, has_side_effects=True, vmem_limit_bytes=60 * 1024 * 1024
        ),
        cost_estimate=pl.CostEstimate(flops=6_000_000_000, bytes_accessed=14_000_000, transcendentals=2_000_000),
    )(hidden, step_slot, positive.reshape(1, CAP), proj)
    for j, part in ((1, part1), (3, part3), (2, part2)):
        ring = [(d, (d // 2 + j) % 4 * 2 + d % 2) for d in range(8)]
        proj_grad = proj_grad + lax.ppermute(part, "rep", ring).astype(F32)
    onehot = (step_slot[None, :] == lax.broadcasted_iota(jnp.int32, (CAP, TOK), 0)).astype(BF16)
    hidden_grad = lax.dot_general(onehot, pooled_grad, (((0,), (0,)), ((), ())), preferred_element_type=F32)
    return (hidden_grad.astype(BF16), proj_grad, loss[0, 0])


def solution(mesh):
    in_specs = (P(("dp", "rep"), None), P(("dp", "rep")), P(("dp", "rep")), P())
    out_specs = (P(("dp", "rep"), None), P(("dp", "rep"), None), P())
    return jax.shard_map(local, mesh=mesh, in_specs=in_specs, out_specs=out_specs, check_vma=False)
```
